128 devices in a mesh: layer: 2 (over core), row: 4 (over z), col: 16 (over x, y).
Axes of the slice: x: 4, y: 4, z: 4, core: 2. Of those that a mesh axis runs over, the one named last changes fastest.
Arguments:
- iterate: bfloat16 [10752, 12288], P(('layer', 'row'), 'col'), parts along dimension 0, may hold values from -0.026062528 to 0.026062528
Outputs:
- update: bfloat16 [10752, 12288], P(('layer', 'row'), 'col'), parts along dimension 0
The draws below stay inside these ranges and needn't reach their ends.
There are 2 independent parts, one for each index of `layer`. The reference program is written for one: setup_inputs(seed, part) draws one part's arguments, and reference() takes and returns one part's arrays. A program takes and returns all parts, laid end to end along the dimension named above; each array names one. Nothing has to cross between parts.
All inputs are finite; a program needn't handle non-finite values.
Results may differ from the reference program's by a relative error of at most 0.024.
Values may be sent and summed in bfloat16 or wider, within the bound.
A program may use at most 128 MiB of HBM per device.

```python
import math
import jax
import jax.numpy as jnp
from jax import lax

M = 5376
N = 12288
N_COL = 16


def draw_iterate(key, part):
    key = jax.random.fold_in(key, 11)
    spread = 1.2 / (math.sqrt(N) + math.sqrt(M))
    values = jax.random.normal(key, (M, N), jnp.float32)
    edge = 4.0 * spread * (1.0 - 1.0 / 200.0)
    return jnp.clip(values * spread, -edge, edge).astype(jnp.bfloat16)


def setup_inputs(seed: int = 0, part: int = 0) -> dict:
    splits = jax.random.split(jax.random.key(seed), 2)
    own_keys = jax.random.split(jax.random.fold_in(splits[1], part), 2)
    return {
        "iterate": draw_iterate(jax.random.fold_in(jax.random.fold_in(splits[1], part), 71), part),
    }


coef_linear = 3.4445
coef_cubic = -4.775
coef_quintic = 2.0315

def reference(iterate):
    block_cols = N // N_COL
    blocks = iterate.reshape(M, N_COL, block_cols).transpose(1, 0, 2)

    def add_block(total, block):
        term = jnp.dot(block, block.T, preferred_element_type=jnp.float32)
        term = lax.optimization_barrier(term.astype(jnp.bfloat16))
        return (total + term.astype(jnp.float32), None)
    gram, unused = lax.scan(add_block, jnp.zeros((M, M), jnp.float32), blocks)
    gram_rounded = gram.astype(jnp.bfloat16)
    gram_square = jnp.dot(gram_rounded, gram_rounded, preferred_element_type=jnp.float32)
    polynomial = (coef_cubic * gram_rounded.astype(jnp.float32) + coef_quintic * gram_square).astype(jnp.bfloat16)
    product = jnp.dot(polynomial, iterate, preferred_element_type=jnp.float32)
    factor = 0.2 * math.sqrt(max(M, N))
    return (factor * (coef_linear * iterate.astype(jnp.float32) + product)).astype(jnp.bfloat16)
```

```python
import math

import jax
import jax.numpy as jnp
from jax import lax
from jax.sharding import PartitionSpec as P

M = 5376
N = 12288


coef_linear = 3.4445
coef_cubic = -4.775
coef_quintic = 2.0315


def on_device(iterate):
    panel = lax.all_gather(iterate, "row", axis=0, tiled=True)
    contract = (((1,), (1,)), ((), ()))
    partial_value = lax.dot_general(
        iterate, panel, contract, preferred_element_type=jnp.float32
    ).astype(jnp.bfloat16)
    gram_rows = lax.psum(partial_value, "col")
    once = jnp.dot(gram_rows, panel, preferred_element_type=jnp.float32)
    once_panel = lax.all_gather(once.astype(jnp.bfloat16), "row", axis=0, tiled=True)
    twice = jnp.dot(gram_rows, once_panel, preferred_element_type=jnp.float32)
    product = coef_cubic * once + coef_quintic * twice
    factor = 0.2 * math.sqrt(max(M, N))
    return (factor * (coef_linear * iterate.astype(jnp.float32) + product)).astype(jnp.bfloat16)


def solution(mesh):
    return jax.shard_map(
        on_device,
        mesh=mesh,
        in_specs=(P(("layer", "row"), "col"),),
        out_specs=P(("layer", "row"), "col"),
        check_vma=False,
    )
```

```python
import functools
import math

import jax
import jax.numpy as jnp
from jax import lax
from jax.experimental import pallas as pl
from jax.experimental.pallas import tpu as pltpu
from jax.sharding import PartitionSpec as P

M = 5376
N = 12288

coef_linear = 3.4445
coef_cubic = -4.775
coef_quintic = 2.0315
factor = 0.2 * math.sqrt(max(M, N))

BLOCK = 1344
CHUNK = 336
DEPTH = 768
WIDE = 1408
PIECE = 384
FULL = 4 * PIECE

PART_A = (0, 176)
PART_B = (176, 160)
HALF_AA = (0, 96)
HALF_AB = (96, 80)
HALF_BA = (176, 80)
HALF_BB = (256, 80)

TRANSPOSED = (((1,), (1,)), ((), ()))
COPIES = 240


def rows_of(part):
    return pl.ds(part[0], part[1])


def kernel(
    x_hbm, o_ref, xs, send, summed, got_far, got_near, got_piece, gram, ys, acc, y_acc,
    local_sem, send_sem, recv_sem,
):
    layer = lax.axis_index("layer")
    row = lax.axis_index("row")
    col = lax.axis_index("col")
    px = lax.div(col, 4)
    py = lax.rem(col, 4)
    pa = px * (1 - layer) + py * layer
    pb = py * (1 - layer) + px * layer

    def ring(position, step):
        return lax.rem(position + (step + 4), 4)

    def device(da=0, db=0, dz=0):
        na, nb = ring(pa, da), ring(pb, db)
        nx = na * (1 - layer) + nb * layer
        ny = nb * (1 - layer) + na * layer
        return (layer, ring(row, dz), nx * 4 + ny)

    used = [0]

    def start(src, dst, target):
        index = used[0]
        used[0] += 1
        copy = pltpu.make_async_remote_copy(
            src_ref=src,
            dst_ref=dst,
            send_sem=send_sem.at[index],
            recv_sem=recv_sem.at[index],
            device_id=target,
            device_id_type=pl.DeviceIdType.MESH,
        )
        copy.start()
        unsent.append(copy)
        return copy

    unsent = []

    def sent(copies):
        for copy in copies:
            copy.wait_send()
            unsent[:] = [other for other in unsent if other is not copy]

    def received(copies):
        for copy in copies:
            copy.wait_recv()

    partners = [device(dz=1), device(dz=-1)]
    for step in (1, 2, 3):
        partners += [device(da=step), device(db=step)]
    barrier = pltpu.get_barrier_semaphore()
    for partner in partners:
        pl.semaphore_signal(
            barrier, inc=1, device_id=partner, device_id_type=pl.DeviceIdType.MESH
        )
    own = pltpu.make_async_copy(x_hbm, xs.at[0], local_sem)
    own.start()
    pl.semaphore_wait(barrier, len(partners))

    low, high = pl.ds(0, BLOCK // 2), pl.ds(BLOCK // 2, BLOCK // 2)
    up_low = start(x_hbm.at[low], xs.at[3, low], device(dz=1))
    down_high = start(x_hbm.at[high], xs.at[1, high], device(dz=-1))
    up_high = start(x_hbm.at[high], xs.at[3, high], device(dz=1))
    down_low = start(x_hbm.at[low], xs.at[1, low], device(dz=-1))

    for k in range(2):
        summed[k, :, pl.ds(1280, FULL - 1280)] = jnp.zeros((CHUNK, FULL - 1280), jnp.bfloat16)
    own.wait()

    def base_a(slot):
        return pl.multiple_of(ring(pa, slot) * CHUNK, 16)

    def base_b(slot):
        return pl.multiple_of(ring(pb, slot) * CHUNK, 16)

    def gram_terms(slot, j):
        mine = jnp.concatenate(
            [
                xs[0, pl.ds(base_a(slot), PART_A[1]), :],
                xs[0, pl.ds(pl.multiple_of(base_b(slot) + PART_B[0], 16), PART_B[1]), :],
            ],
            axis=0,
        )
        return lax.dot_general(mine, xs[j], TRANSPOSED, preferred_element_type=jnp.float32)

    buffer_set = {0: 0, 1: 1, 3: 0, 2: 1}
    landing_set = {0: 0, 1: 1, 3: 2, 2: 0}
    from_buffer = {}
    step1, step2, step3, step4, step5, step6 = {}, {}, {}, {}, {}, {}
    body = pl.ds(0, BLOCK)
    wide = pl.ds(0, WIDE)

    def reuse(name, k):
        sent(from_buffer.pop((name, k), []))

    def phase1(j):
        k, q = buffer_set[j], landing_set[j]
        reuse("far", k)
        send[k, 0, :, body] = gram_terms(2, j).astype(jnp.bfloat16)
        step1[j] = []
        for half, target in (
            (HALF_AA, device(da=1)),
            (HALF_BA, device(db=1)),
            (HALF_AB, device(da=-1)),
            (HALF_BB, device(db=-1)),
        ):
            rows = rows_of(half)
            step1[j].append(start(send.at[k, 0, rows], got_far.at[q, rows], target))
        from_buffer["far", k] = list(step1[j])

    def phase2(j):
        k, q = buffer_set[j], landing_set[j]
        received(step1[j])
        step2[j] = []
        for side, slot, added in ((1, 1, (HALF_AA, HALF_BA)), (2, 3, (HALF_AB, HALF_BB))):
            reuse(side, k)
            terms = gram_terms(slot, j)
            for half in (HALF_AA, HALF_AB, HALF_BA, HALF_BB):
                rows = rows_of(half)
                value = terms[half[0] : half[0] + half[1], :]
                if half in added:
                    value = value + got_far[q, rows, body].astype(jnp.float32)
                send[k, side, rows, body] = value.astype(jnp.bfloat16)
            way = 1 if slot == 1 else -1
            copies = []
            for part, target in ((PART_A, device(da=way)), (PART_B, device(db=way))):
                rows = rows_of(part)
                copies.append(
                    start(send.at[k, side, rows], got_near.at[q, side - 1, rows], target)
                )
            from_buffer[side, k] = copies
            step2[j] += copies

    def piece(position):
        return pl.ds(pl.multiple_of(position * PIECE, 128), PIECE)

    def phase3(j):
        k, q = buffer_set[j], landing_set[j]
        terms = gram_terms(0, j)
        received(step2[j])
        reuse("sum", k)
        summed[k, :, body] = (
            terms
            + got_near[q, 0, :, body].astype(jnp.float32)
            + got_near[q, 1, :, body].astype(jnp.float32)
        ).astype(jnp.bfloat16)
        step3[j] = []
        for step in (2, 1, 3):
            for part, place, target in (
                (PART_A, ring(pb, step), device(db=step)),
                (PART_B, ring(pa, step), device(da=step)),
            ):
                rows = rows_of(part)
                step3[j].append(
                    start(
                        summed.at[k, rows, piece(place)],
                        got_piece.at[q, step - 1, rows],
                        target,
                    )
                )
        from_buffer["sum", k] = list(step3[j])

    def phase4(j):
        k, q = buffer_set[j], landing_set[j]
        received(step3[j])
        for part, place in ((PART_A, pb), (PART_B, pa)):
            rows = rows_of(part)
            value = summed[k, rows, piece(place)].astype(jnp.float32)
            for step in range(3):
                value = value + got_piece[q, step, rows, :].astype(jnp.float32)
            gram[0, j, rows, piece(place)] = value.astype(jnp.bfloat16)
        step4[j] = []
        for step in (2, 1, 3):
            for part, place, target in (
                (PART_A, pb, device(db=step)),
                (PART_B, pa, device(da=step)),
            ):
                where = gram.at[0, j, rows_of(part), piece(place)]
                step4[j].append(start(where, where, target))

    def phase5(j, half):
        if half == 0:
            received(step4[j])
            step5[j] = []
        copies = []
        for rows_half, target_up, target_down in (
            ((HALF_AA, HALF_AB)[half], device(da=1), device(da=-1)),
            ((HALF_BA, HALF_BB)[half], device(db=1), device(db=-1)),
        ):
            rows = rows_of(rows_half)
            src = gram.at[0, j, rows, wide]
            copies.append(start(src, gram.at[3, j, rows, wide], target_up))
            copies.append(start(src, gram.at[1, j, rows, wide], target_down))
        step5[j].append(copies)

    def phase6(j, half):
        received(step5[j][half])
        if half == 0:
            step6[j] = []
        for rows_half, target in (
            ((HALF_AA, HALF_AB)[half], device(da=(1, -1)[half])),
            ((HALF_BA, HALF_BB)[half], device(db=(1, -1)[half])),
        ):
            rows = rows_of(rows_half)
            step6[j].append(
                start(
                    gram.at[(3, 1)[half], j, rows, wide], gram.at[2, j, rows, wide], target
                )
            )

    def place_of(slot, part):
        base = base_a(slot) if part[0] < PART_B[0] else base_b(slot)
        return pl.ds(pl.multiple_of(base + part[0], 16), part[1])

    direct, forward = {}, {}

    def once(name, pieces):
        total = sum(part[1] for _, part in pieces)

        def add(j, carry):
            left = [gram[slot, j, rows_of(part), body] for slot, part in pieces]
            left = left[0] if len(left) == 1 else jnp.concatenate(left, axis=0)
            term = jnp.dot(left, xs[j], preferred_element_type=jnp.float32)

            @pl.when(j == 0)
            def _():
                y_acc[pl.ds(0, total), :] = term

            @pl.when(j != 0)
            def _():
                y_acc[pl.ds(0, total), :] += term

            return carry

        lax.fori_loop(0, 4, add, 0)
        offset = 0
        for slot, part in pieces:
            value = y_acc[pl.ds(offset, part[1]), :]
            offset += part[1]
            place = place_of(slot, part)
            acc[slot, rows_of(part), :] = (
                coef_linear * xs[0, place, :].astype(jnp.float32) + coef_cubic * value
            )
            ys[0, place, :] = value.astype(jnp.bfloat16)
        direct[name] = []
        for slot, part in pieces:
            place = place_of(slot, part)
            src = ys.at[0, place]
            direct[name].append(
                (
                    slot,
                    part,
                    start(src, ys.at[3, place], device(dz=1)),
                    start(src, ys.at[1, place], device(dz=-1)),
                )
            )

    def pass_on(name):
        forward[name] = []
        for slot, part, up, down in direct[name]:
            place = place_of(slot, part)
            received([up, down])
            if part[0] < PART_B[0]:
                copy = start(ys.at[3, place], ys.at[2, place], device(dz=1))
            else:
                copy = start(ys.at[1, place], ys.at[2, place], device(dz=-1))
            forward[name].append(copy)

    def twice(j, last=False):
        def add(slot, carry):
            term = jnp.dot(gram[slot, j, :, body], ys[j], preferred_element_type=jnp.float32)
            value = acc[slot] + coef_quintic * term
            if last:
                value = (factor * value).astype(jnp.bfloat16)
                for part in (PART_A, PART_B):
                    o_ref[place_of(slot, part), :] = value[part[0] : part[0] + part[1], :]
            else:
                acc[slot] = value
            return carry

        lax.fori_loop(0, 4, add, 0)

    phase1(0)
    phase2(0)
    phase3(0)
    phase4(0)
    received([up_low])
    far_low = start(xs.at[3, low], xs.at[2, low], device(dz=1))
    received([down_high])
    far_high = start(xs.at[1, high], xs.at[2, high], device(dz=-1))
    phase5(0, 0)
    phase5(0, 1)
    phase6(0, 0)
    phase6(0, 1)
    received([down_low])
    phase1(1)
    received([up_high])
    phase1(3)
    phase2(1)
    phase2(3)
    received([far_low, far_high])
    phase1(2)
    phase3(1)
    phase3(3)
    phase2(2)
    phase4(1)
    phase4(3)
    phase3(2)
    phase5(1, 0)
    phase5(3, 0)
    phase4(2)
    received(step6[0])
    phase5(2, 0)
    phase5(1, 1)
    phase5(3, 1)
    phase5(2, 1)
    once("own", ((0, PART_A), (0, PART_B)))
    phase6(1, 0)
    phase6(3, 0)
    phase6(2, 0)
    once("first", ((1, HALF_AA), (3, HALF_AA), (1, HALF_BA), (3, HALF_BA)))
    pass_on("own")
    phase6(1, 1)
    phase6(3, 1)
    phase6(2, 1)
    once("second", ((1, HALF_AB), (3, HALF_AB), (1, HALF_BB), (3, HALF_BB)))
    pass_on("first")
    for j in (1, 3, 2):
        received(step6[j])
    once("last", ((2, PART_A), (2, PART_B)))
    pass_on("second")
    twice(0)
    pass_on("last")
    twice(1)
    twice(3)
    for name in ("own", "first", "second", "last"):
        received(forward[name])
    twice(2, last=True)
    sent(list(unsent))


def on_device(iterate):
    any_space = pl.BlockSpec(memory_space=pl.ANY)
    vmem = pl.BlockSpec(memory_space=pltpu.VMEM)
    bf16 = jnp.bfloat16
    return pl.pallas_call(
        kernel,
        out_shape=jax.ShapeDtypeStruct((BLOCK, DEPTH), bf16),
        in_specs=[any_space],
        out_specs=vmem,
        scratch_shapes=[
            pltpu.VMEM((4, BLOCK, DEPTH), bf16),
            pltpu.VMEM((2, 3, CHUNK, WIDE), bf16),
            pltpu.VMEM((2, CHUNK, FULL), bf16),
            pltpu.VMEM((3, CHUNK, WIDE), bf16),
            pltpu.VMEM((3, 2, CHUNK, WIDE), bf16),
            pltpu.VMEM((3, 3, CHUNK, PIECE), bf16),
            pltpu.VMEM((4, 4, CHUNK, FULL), bf16),
            pltpu.VMEM((4, BLOCK, DEPTH), bf16),
            pltpu.VMEM((4, CHUNK, DEPTH), jnp.float32),
            pltpu.VMEM((352, DEPTH), jnp.float32),
            pltpu.SemaphoreType.DMA,
            pltpu.SemaphoreType.DMA((COPIES,)),
            pltpu.SemaphoreType.DMA((COPIES,)),
        ],
        compiler_params=pltpu.CompilerParams(
            collective_id=0, has_side_effects=True, vmem_limit_bytes=63 * 2**20
        ),
        name="newton_schulz",
    )(iterate)


def solution(mesh):
    return jax.shard_map(
        on_device,
        mesh=mesh,
        in_specs=(P(("layer", "row"), "col"),),
        out_specs=P(("layer", "row"), "col"),
        check_vma=False,
    )
```

```python
import functools
import math

import jax
import jax.numpy as jnp
from jax import lax
from jax.experimental import pallas as pl
from jax.experimental.pallas import tpu as pltpu
from jax.sharding import PartitionSpec as P

M = 5376
N = 12288

coef_linear = 3.4445
coef_cubic = -4.775
coef_quintic = 2.0315
factor = 0.2 * math.sqrt(max(M, N))

BLOCK = 1344
CHUNK = 336
SPLIT = 640
DEPTH = 768
WIDE = 1408
PIECE = 384
FULL = 4 * PIECE

PART_A = (0, 176)
PART_B = (176, 160)
HALF_AA = (0, 96)
HALF_AB = (96, 80)
HALF_BA = (176, 80)
HALF_BB = (256, 80)

TRANSPOSED = (((1,), (1,)), ((), ()))
LEFT_TRANSPOSED = (((0,), (0,)), ((), ()))
COPIES = 200


def rows_of(part):
    return pl.ds(part[0], part[1])


def kernel(
    x_hbm, o_ref, xs, send, summed, got_far, got_near, got_piece, gram, ys, acc, y_acc,
    local_sem, send_sem, recv_sem,
):
    layer = lax.axis_index("layer")
    row = lax.axis_index("row")
    col = lax.axis_index("col")
    px = lax.div(col, 4)
    py = lax.rem(col, 4)
    pa = px * (1 - layer) + py * layer
    pb = py * (1 - layer) + px * layer

    def ring(position, step):
        return lax.rem(position + (step + 4), 4)

    def device(da=0, db=0, dz=0):
        na, nb = ring(pa, da), ring(pb, db)
        nx = na * (1 - layer) + nb * layer
        ny = nb * (1 - layer) + na * layer
        return (layer, ring(row, dz), nx * 4 + ny)

    used = [0]

    def start(src, dst, target):
        index = used[0]
        used[0] += 1
        copy = pltpu.make_async_remote_copy(
            src_ref=src,
            dst_ref=dst,
            send_sem=send_sem.at[index],
            recv_sem=recv_sem.at[index],
            device_id=target,
            device_id_type=pl.DeviceIdType.MESH,
        )
        copy.start()
        unsent.append(copy)
        return copy

    unsent = []

    def sent(copies):
        for copy in copies:
            copy.wait_send()
            unsent[:] = [other for other in unsent if other is not copy]

    def received(copies):
        for copy in copies:
            copy.wait_recv()

    partners = [device(dz=1), device(dz=-1)]
    for step in (1, 2, 3):
        partners += [device(da=step), device(db=step)]
    barrier = pltpu.get_barrier_semaphore()
    for partner in partners:
        pl.semaphore_signal(
            barrier, inc=1, device_id=partner, device_id_type=pl.DeviceIdType.MESH
        )
    own = pltpu.make_async_copy(x_hbm, xs.at[0], local_sem)
    own.start()
    pl.semaphore_wait(barrier, len(partners))

    low, high = pl.ds(0, SPLIT), pl.ds(SPLIT, BLOCK - SPLIT)
    down_low = start(x_hbm.at[low], xs.at[1, low], device(dz=-1))
    up_high = start(x_hbm.at[high], xs.at[3, high], device(dz=1))
    down_high = start(x_hbm.at[high], xs.at[1, high], device(dz=-1))

    for k in range(2):
        summed[k, :, pl.ds(1280, FULL - 1280)] = jnp.zeros((CHUNK, FULL - 1280), jnp.bfloat16)
    own.wait()

    def place_of(slot, part):
        position = pa if part[0] < PART_B[0] else pb
        return pl.ds(pl.multiple_of(ring(position, slot) * CHUNK + part[0], 16), part[1])

    def slot_rows(ref, j, slot):
        return jnp.concatenate(
            [ref[j, place_of(slot, PART_A), :], ref[j, place_of(slot, PART_B), :]], axis=0
        )

    def gram_terms(slot, j, columns):
        return lax.dot_general(
            slot_rows(xs, 0, slot), xs[j, columns, :], TRANSPOSED,
            preferred_element_type=jnp.float32,
        )

    buffer_set = {0: 0, 1: 1, 2: 0}
    from_buffer = {}
    step1, step2, step3, step4, step5, step6 = {}, {}, {}, {}, {}, {}
    body = pl.ds(0, BLOCK)
    wide = pl.ds(0, WIDE)
    halves = (low, high)
    wide_halves = (low, pl.ds(SPLIT, WIDE - SPLIT))

    def reuse(name, j):
        key = name, buffer_set[j]
        owner, copies = from_buffer.get(key, (j, []))
        if owner != j:
            sent(copies)
            copies = []
        from_buffer[key] = (j, copies)
        return copies

    def phase1(j, h):
        k = buffer_set[j]
        copies = reuse("far", j)
        send[k, 0, :, halves[h]] = gram_terms(2, j, halves[h]).astype(jnp.bfloat16)
        step1[j, h] = []
        for half, target in (
            (HALF_AA, device(da=1)),
            (HALF_BA, device(db=1)),
            (HALF_AB, device(da=-1)),
            (HALF_BB, device(db=-1)),
        ):
            rows = rows_of(half)
            step1[j, h].append(
                start(
                    send.at[k, 0, rows, wide_halves[h]],
                    got_far.at[k, rows, wide_halves[h]],
                    target,
                )
            )
        copies += step1[j, h]

    def phase2(j, h):
        k = buffer_set[j]
        received(step1[j, h])
        step2[j, h] = []
        for side, slot, added in ((1, 1, (HALF_AA, HALF_BA)), (2, 3, (HALF_AB, HALF_BB))):
            copies = reuse(side, j)
            terms = gram_terms(slot, j, halves[h])
            for half in (HALF_AA, HALF_AB, HALF_BA, HALF_BB):
                rows = rows_of(half)
                value = terms[half[0] : half[0] + half[1], :]
                if half in added:
                    value = value + got_far[k, rows, halves[h]].astype(jnp.float32)
                send[k, side, rows, halves[h]] = value.astype(jnp.bfloat16)
            way = 1 if slot == 1 else -1
            for part, target in ((PART_A, device(da=way)), (PART_B, device(db=way))):
                rows = rows_of(part)
                copy = start(
                    send.at[k, side, rows, wide_halves[h]],
                    got_near.at[k, side - 1, rows, wide_halves[h]],
                    target,
                )
                copies.append(copy)
                step2[j, h].append(copy)

    def piece(position):
        return pl.ds(pl.multiple_of(position * PIECE, 128), PIECE)

    def phase3(j):
        k = buffer_set[j]
        copies = reuse("sum", j)
        for h in (0, 1):
            terms = gram_terms(0, j, halves[h])
            received(step2[j, h])
            summed[k, :, halves[h]] = (
                terms
                + got_near[k, 0, :, halves[h]].astype(jnp.float32)
                + got_near[k, 1, :, halves[h]].astype(jnp.float32)
            ).astype(jnp.bfloat16)
        step3[j] = []
        for step in (2, 1, 3):
            for part, place, target in (
                (PART_A, ring(pb, step), device(db=step)),
                (PART_B, ring(pa, step), device(da=step)),
            ):
                rows = rows_of(part)
                step3[j].append(
                    start(
                        summed.at[k, rows, piece(place)],
                        got_piece.at[k, step - 1, rows],
                        target,
                    )
                )
        copies += step3[j]

    def spread(j):
        step4[j] = []
        for step in (2, 1, 3):
            for part, place, target in (
                (PART_A, pb, device(db=step)),
                (PART_B, pa, device(da=step)),
            ):
                where = gram.at[0, j, rows_of(part), piece(place)]
                step4[j].append(start(where, where, target))

    def phase4(j):
        k = buffer_set[j]
        received(step3[j])
        for part, place in ((PART_A, pb), (PART_B, pa)):
            rows = rows_of(part)
            value = summed[k, rows, piece(place)].astype(jnp.float32)
            for step in range(3):
                value = value + got_piece[k, step, rows, :].astype(jnp.float32)
            gram[0, j, rows, piece(place)] = value.astype(jnp.bfloat16)
        if j == 1:
            for part, place in ((PART_A, pb), (PART_B, pa)):
                rows = rows_of(part)
                mirrored.append(
                    start(
                        gram.at[0, 1, rows, piece(place)],
                        gram.at[0, 3, rows, piece(place)],
                        device(dz=1),
                    )
                )
        spread(j)

    mirrored = []

    def phase5(j, half):
        if half == 0:
            received(step4[j])
            step5[j] = []
        copies = []
        for rows_half, target_up, target_down in (
            ((HALF_AA, HALF_AB)[half], device(da=1), device(da=-1)),
            ((HALF_BA, HALF_BB)[half], device(db=1), device(db=-1)),
        ):
            rows = rows_of(rows_half)
            src = gram.at[0, j, rows, wide]
            copies.append(start(src, gram.at[3, j, rows, wide], target_up))
            copies.append(start(src, gram.at[1, j, rows, wide], target_down))
        step5[j].append(copies)

    def phase6(j, half):
        received(step5[j][half])
        if half == 0:
            step6[j] = []
        for rows_half, target in (
            ((HALF_AA, HALF_AB)[half], device(da=(1, -1)[half])),
            ((HALF_BA, HALF_BB)[half], device(db=(1, -1)[half])),
        ):
            rows = rows_of(rows_half)
            step6[j].append(
                start(
                    gram.at[(3, 1)[half], j, rows, wide], gram.at[2, j, rows, wide], target
                )
            )

    direct, forward = {}, {}

    def mirrored_terms(slot, ref):
        return lax.dot_general(
            gram[slot, 3, :, body], slot_rows(ref, 3, slot), LEFT_TRANSPOSED,
            preferred_element_type=jnp.float32,
        )

    def once_mirrored():
        acc[...] = mirrored_terms(0, xs)

        def add(slot, carry):
            acc[...] += mirrored_terms(slot, xs)
            return carry

        lax.fori_loop(1, 4, add, 0)

    def once(name, pieces):
        total = sum(part[1] for _, part in pieces)

        def terms(j):
            left = [gram[slot, j, rows_of(part), body] for slot, part in pieces]
            left = left[0] if len(left) == 1 else jnp.concatenate(left, axis=0)
            return jnp.dot(left, xs[j], preferred_element_type=jnp.float32)

        y_acc[pl.ds(0, total), :] = terms(0)

        def add(j, carry):
            y_acc[pl.ds(0, total), :] += terms(j)
            return carry

        lax.fori_loop(1, 3, add, 0)
        offset = 0
        for slot, part in pieces:
            place = place_of(slot, part)
            value = y_acc[pl.ds(offset, part[1]), :] + acc[place, :]
            offset += part[1]
            acc[place, :] = coef_linear * xs[0, place, :].astype(jnp.float32) + coef_cubic * value
            ys[0, place, :] = value.astype(jnp.bfloat16)
        direct[name] = []
        for slot, part in pieces:
            place = place_of(slot, part)
            src = ys.at[0, place]
            direct[name].append(
                (
                    slot,
                    part,
                    start(src, ys.at[3, place], device(dz=1)),
                    start(src, ys.at[1, place], device(dz=-1)),
                )
            )

    def pass_on(name):
        forward[name] = []
        for slot, part, up, down in direct[name]:
            place = place_of(slot, part)
            received([up, down])
            if part[0] < PART_B[0]:
                copy = start(ys.at[3, place], ys.at[2, place], device(dz=1))
            else:
                copy = start(ys.at[1, place], ys.at[2, place], device(dz=-1))
            forward[name].append(copy)

    def twice(j, last=False):
        def add(slot, carry):
            term = coef_quintic * jnp.dot(
                gram[slot, j, :, body], ys[j], preferred_element_type=jnp.float32
            )
            for part in (PART_A, PART_B):
                place = place_of(slot, part)
                value = acc[place, :] + term[part[0] : part[0] + part[1], :]
                if last:
                    o_ref[place, :] = (factor * value).astype(jnp.bfloat16)
                else:
                    acc[place, :] = value
            return carry

        lax.fori_loop(0, 4, add, 0)

    def twice_mirrored():
        def add(slot, carry):
            acc[...] += coef_quintic * mirrored_terms(slot, ys)
            return carry

        lax.fori_loop(0, 4, add, 0)

    phase1(0, 0)
    phase1(0, 1)
    phase2(0, 0)
    phase2(0, 1)
    phase3(0)
    received([down_low])
    far_low = start(xs.at[1, low], xs.at[2, low], device(dz=-1))
    phase1(1, 0)
    received([up_high])
    far_high = start(xs.at[3, high], xs.at[2, high], device(dz=1))
    up_low = start(x_hbm.at[low], xs.at[3, low], device(dz=1))
    phase4(0)
    phase2(1, 0)
    phase5(0, 0)
    phase5(0, 1)
    received([down_high])
    phase1(1, 1)
    phase6(0, 0)
    phase6(0, 1)
    received([far_high])
    phase1(2, 1)
    phase2(1, 1)
    phase3(1)
    phase2(2, 1)
    phase4(1)
    received([far_low])
    phase1(2, 0)
    received(mirrored)
    spread(3)
    phase2(2, 0)
    phase5(3, 0)
    phase5(3, 1)
    phase3(2)
    phase6(3, 0)
    phase6(3, 1)
    phase4(2)
    phase5(1, 0)
    phase5(1, 1)
    received([up_low])
    received(step6[3])
    once_mirrored()
    phase5(2, 0)
    phase5(2, 1)
    received(step6[0])
    once("own", ((0, PART_A), (0, PART_B)))
    phase6(1, 0)
    phase6(2, 0)
    once("first", ((1, HALF_AA), (3, HALF_AA), (1, HALF_BA), (3, HALF_BA)))
    pass_on("own")
    phase6(1, 1)
    phase6(2, 1)
    once("second", ((1, HALF_AB), (3, HALF_AB), (1, HALF_BB), (3, HALF_BB)))
    pass_on("first")
    received(step6[1])
    received(step6[2])
    once("last", ((2, PART_A), (2, PART_B)))
    pass_on("second")
    twice(0)
    pass_on("last")
    twice_mirrored()
    twice(1)
    for name in ("own", "first", "second", "last"):
        received(forward[name])
    twice(2, last=True)
    sent(list(unsent))


def on_device(iterate):
    any_space = pl.BlockSpec(memory_space=pl.ANY)
    vmem = pl.BlockSpec(memory_space=pltpu.VMEM)
    bf16 = jnp.bfloat16
    return pl.pallas_call(
        kernel,
        out_shape=jax.ShapeDtypeStruct((BLOCK, DEPTH), bf16),
        in_specs=[any_space],
        out_specs=vmem,
        scratch_shapes=[
            pltpu.VMEM((4, BLOCK, DEPTH), bf16),
            pltpu.VMEM((2, 3, CHUNK, WIDE), bf16),
            pltpu.VMEM((2, CHUNK, FULL), bf16),
            pltpu.VMEM((2, CHUNK, WIDE), bf16),
            pltpu.VMEM((2, 2, CHUNK, WIDE), bf16),
            pltpu.VMEM((2, 3, CHUNK, PIECE), bf16),
            pltpu.VMEM((4, 4, CHUNK, FULL), bf16),
            pltpu.VMEM((4, BLOCK, DEPTH), bf16),
            pltpu.VMEM((BLOCK, DEPTH), jnp.float32),
            pltpu.VMEM((352, DEPTH), jnp.float32),
            pltpu.SemaphoreType.DMA,
            pltpu.SemaphoreType.DMA((COPIES,)),
            pltpu.SemaphoreType.DMA((COPIES,)),
        ],
        compiler_params=pltpu.CompilerParams(
            collective_id=0, has_side_effects=True, vmem_limit_bytes=63 * 2**20
        ),
        name="newton_schulz",
    )(iterate)


def solution(mesh):
    return jax.shard_map(
        on_device,
        mesh=mesh,
        in_specs=(P(("layer", "row"), "col"),),
        out_specs=P(("layer", "row"), "col"),
        check_vma=False,
    )
```

```python
import functools
import math

import jax
import jax.numpy as jnp
from jax import lax
from jax.experimental import pallas as pl
from jax.experimental.pallas import tpu as pltpu
from jax.sharding import PartitionSpec as P

M = 5376
N = 12288

coef_linear = 3.4445
coef_cubic = -4.775
coef_quintic = 2.0315
factor = 0.2 * math.sqrt(max(M, N))

BLOCK = 1344
CHUNK = 336
SPLIT = 640
DEPTH = 768
WIDE = 1408
PIECE = 384
FULL = 4 * PIECE

PART_A = (0, 176)
PART_B = (176, 160)
HALF_AA = (0, 96)
HALF_AB = (96, 80)
HALF_BA = (176, 80)
HALF_BB = (256, 80)

TRANSPOSED = (((1,), (1,)), ((), ()))
LEFT_TRANSPOSED = (((0,), (0,)), ((), ()))
COPIES = 200


def rows_of(part):
    return pl.ds(part[0], part[1])


def kernel(
    x_hbm, o_ref, xs, send, summed, got_far, got_near, got_piece, handed, gram, ys, acc, y_acc,
    local_sem, send_sem, recv_sem,
):
    layer = lax.axis_index("layer")
    row = lax.axis_index("row")
    col = lax.axis_index("col")
    px = lax.div(col, 4)
    py = lax.rem(col, 4)
    pa = px * (1 - layer) + py * layer
    pb = py * (1 - layer) + px * layer

    def ring(position, step):
        return lax.rem(position + (step + 4), 4)

    def device(da=0, db=0, dz=0):
        na, nb = ring(pa, da), ring(pb, db)
        nx = na * (1 - layer) + nb * layer
        ny = nb * (1 - layer) + na * layer
        return (layer, ring(row, dz), nx * 4 + ny)

    used = [0]

    def start(src, dst, target):
        index = used[0]
        used[0] += 1
        copy = pltpu.make_async_remote_copy(
            src_ref=src,
            dst_ref=dst,
            send_sem=send_sem.at[index],
            recv_sem=recv_sem.at[index],
            device_id=target,
            device_id_type=pl.DeviceIdType.MESH,
        )
        copy.start()
        unsent.append(copy)
        return copy

    unsent = []

    def sent(copies):
        for copy in copies:
            copy.wait_send()
            unsent[:] = [other for other in unsent if other is not copy]

    def received(copies):
        for copy in copies:
            copy.wait_recv()

    partners = [device(dz=1), device(dz=-1)]
    for step in (1, 2, 3):
        partners += [device(da=step), device(db=step)]
    barrier = pltpu.get_barrier_semaphore()
    for partner in partners:
        pl.semaphore_signal(
            barrier, inc=1, device_id=partner, device_id_type=pl.DeviceIdType.MESH
        )
    own = pltpu.make_async_copy(x_hbm, xs.at[0], local_sem)
    own.start()
    pl.semaphore_wait(barrier, len(partners))

    low, high = pl.ds(0, SPLIT), pl.ds(SPLIT, BLOCK - SPLIT)
    down_low = start(x_hbm.at[low], xs.at[1, low], device(dz=-1))
    up_high = start(x_hbm.at[high], xs.at[3, high], device(dz=1))
    down_high = start(x_hbm.at[high], xs.at[1, high], device(dz=-1))
    up_low = start(x_hbm.at[low], xs.at[3, low], device(dz=1))

    for k in range(2):
        summed[k, :, pl.ds(1280, FULL - 1280)] = jnp.zeros((CHUNK, FULL - 1280), jnp.bfloat16)
    own.wait()

    def place_of(slot, part):
        position = pa if part[0] < PART_B[0] else pb
        return pl.ds(pl.multiple_of(ring(position, slot) * CHUNK + part[0], 16), part[1])

    def slot_rows(ref, j, slot):
        return jnp.concatenate(
            [ref[j, place_of(slot, PART_A), :], ref[j, place_of(slot, PART_B), :]], axis=0
        )

    def gram_terms(slot, j, columns):
        left, right = (3, 1) if j == 2 else (0, j)
        return lax.dot_general(
            slot_rows(xs, left, slot), xs[right, columns, :], TRANSPOSED,
            preferred_element_type=jnp.float32,
        )

    buffer_set = {0: 0, 1: 1, 2: 0}
    from_buffer = {}
    step1, step2, step3, step4, step5, step6 = {}, {}, {}, {}, {}, {}
    body = pl.ds(0, BLOCK)
    wide = pl.ds(0, WIDE)
    halves = (low, high)
    wide_halves = (low, pl.ds(SPLIT, WIDE - SPLIT))

    def reuse(name, j):
        key = name, buffer_set[j]
        owner, copies = from_buffer.get(key, (j, []))
        if owner != j:
            sent(copies)
            copies = []
        from_buffer[key] = (j, copies)
        return copies

    def phase1(j, h):
        k = buffer_set[j]
        copies = reuse("far", j)
        send[k, 0, :, halves[h]] = gram_terms(2, j, halves[h]).astype(jnp.bfloat16)
        step1[j, h] = []
        for half, target in (
            (HALF_AA, device(da=1)),
            (HALF_BA, device(db=1)),
            (HALF_AB, device(da=-1)),
            (HALF_BB, device(db=-1)),
        ):
            rows = rows_of(half)
            step1[j, h].append(
                start(
                    send.at[k, 0, rows, wide_halves[h]],
                    got_far.at[k, rows, wide_halves[h]],
                    target,
                )
            )
        copies += step1[j, h]

    def phase2(j, h):
        k = buffer_set[j]
        received(step1[j, h])
        step2[j, h] = []
        for side, slot, added in ((1, 1, (HALF_AA, HALF_BA)), (2, 3, (HALF_AB, HALF_BB))):
            copies = reuse(side, j)
            terms = gram_terms(slot, j, halves[h])
            for half in (HALF_AA, HALF_AB, HALF_BA, HALF_BB):
                rows = rows_of(half)
                value = terms[half[0] : half[0] + half[1], :]
                if half in added:
                    value = value + got_far[k, rows, halves[h]].astype(jnp.float32)
                send[k, side, rows, halves[h]] = value.astype(jnp.bfloat16)
            way = 1 if slot == 1 else -1
            for part, target in ((PART_A, device(da=way)), (PART_B, device(db=way))):
                rows = rows_of(part)
                copy = start(
                    send.at[k, side, rows, wide_halves[h]],
                    got_near.at[k, side - 1, rows, wide_halves[h]],
                    target,
                )
                copies.append(copy)
                step2[j, h].append(copy)

    def piece(position):
        return pl.ds(pl.multiple_of(position * PIECE, 128), PIECE)

    def phase3(j):
        k = buffer_set[j]
        copies = reuse("sum", j)
        for h in (0, 1):
            terms = gram_terms(0, j, halves[h])
            received(step2[j, h])
            summed[k, :, halves[h]] = (
                terms
                + got_near[k, 0, :, halves[h]].astype(jnp.float32)
                + got_near[k, 1, :, halves[h]].astype(jnp.float32)
            ).astype(jnp.bfloat16)
        step3[j] = []
        for step in (2, 1, 3):
            for part, place, target in (
                (PART_A, ring(pb, step), device(db=step)),
                (PART_B, ring(pa, step), device(da=step)),
            ):
                rows = rows_of(part)
                step3[j].append(
                    start(
                        summed.at[k, rows, piece(place)],
                        got_piece.at[k, step - 1, rows],
                        target,
                    )
                )
        copies += step3[j]

    def spread(j):
        step4[j] = []
        for step in (2, 1, 3):
            for part, place, target in (
                (PART_A, pb, device(db=step)),
                (PART_B, pa, device(da=step)),
            ):
                where = gram.at[0, j, rows_of(part), piece(place)]
                step4[j].append(start(where, where, target))

    def phase4(j):
        k = buffer_set[j]
        received(step3[j])
        for part, place in ((PART_A, pb), (PART_B, pa)):
            rows = rows_of(part)
            value = summed[k, rows, piece(place)].astype(jnp.float32)
            for step in range(3):
                value = value + got_piece[k, step, rows, :].astype(jnp.float32)
            value = value.astype(jnp.bfloat16)
            if j == 2:
                handed[rows, :] = value
            else:
                gram[0, j, rows, piece(place)] = value
        if j != 0:
            shared[j] = []
            for part, place in ((PART_A, pb), (PART_B, pa)):
                rows = rows_of(part)
                if j == 1:
                    src, theirs, way = gram.at[0, 1, rows, piece(place)], 3, 1
                else:
                    src, theirs, way = handed.at[rows], 2, -1
                shared[j].append(
                    start(src, gram.at[0, theirs, rows, piece(place)], device(dz=way))
                )
        if j != 2:
            spread(j)

    shared = {}

    def phase5(j, half):
        if half == 0:
            received(step4[j])
            step5[j] = []
        copies = []
        for rows_half, target_up, target_down in (
            ((HALF_AA, HALF_AB)[half], device(da=1), device(da=-1)),
            ((HALF_BA, HALF_BB)[half], device(db=1), device(db=-1)),
        ):
            rows = rows_of(rows_half)
            src = gram.at[0, j, rows, wide]
            copies.append(start(src, gram.at[3, j, rows, wide], target_up))
            copies.append(start(src, gram.at[1, j, rows, wide], target_down))
        step5[j].append(copies)

    def phase6(j, half):
        received(step5[j][half])
        if half == 0:
            step6[j] = []
        for rows_half, target in (
            ((HALF_AA, HALF_AB)[half], device(da=(1, -1)[half])),
            ((HALF_BA, HALF_BB)[half], device(db=(1, -1)[half])),
        ):
            rows = rows_of(rows_half)
            step6[j].append(
                start(
                    gram.at[(3, 1)[half], j, rows, wide], gram.at[2, j, rows, wide], target
                )
            )

    direct, forward = {}, {}

    def mirrored_terms(slot, ref):
        return lax.dot_general(
            gram[slot, 3, :, body], slot_rows(ref, 3, slot), LEFT_TRANSPOSED,
            preferred_element_type=jnp.float32,
        )

    def once_mirrored():
        acc[...] = mirrored_terms(0, xs)

        def add(slot, carry):
            acc[...] += mirrored_terms(slot, xs)
            return carry

        lax.fori_loop(1, 4, add, 0)

    def once(name, pieces):
        total = sum(part[1] for _, part in pieces)

        def terms(j):
            left = [gram[slot, j, rows_of(part), body] for slot, part in pieces]
            left = left[0] if len(left) == 1 else jnp.concatenate(left, axis=0)
            return jnp.dot(left, xs[j], preferred_element_type=jnp.float32)

        y_acc[pl.ds(0, total), :] = terms(0)

        def add(j, carry):
            y_acc[pl.ds(0, total), :] += terms(j)
            return carry

        lax.fori_loop(1, 3, add, 0)
        offset = 0
        for slot, part in pieces:
            place = place_of(slot, part)
            value = y_acc[pl.ds(offset, part[1]), :] + acc[place, :]
            offset += part[1]
            acc[place, :] = coef_linear * xs[0, place, :].astype(jnp.float32) + coef_cubic * value
            ys[0, place, :] = value.astype(jnp.bfloat16)
        direct[name] = []
        for slot, part in pieces:
            place = place_of(slot, part)
            src = ys.at[0, place]
            direct[name].append(
                (
                    slot,
                    part,
                    start(src, ys.at[3, place], device(dz=1)),
                    start(src, ys.at[1, place], device(dz=-1)),
                )
            )

    def pass_on(name):
        forward[name] = []
        for slot, part, up, down in direct[name]:
            place = place_of(slot, part)
            received([up, down])
            if part[0] < PART_B[0]:
                copy = start(ys.at[3, place], ys.at[2, place], device(dz=1))
            else:
                copy = start(ys.at[1, place], ys.at[2, place], device(dz=-1))
            forward[name].append(copy)

    def twice(j, last=False):
        def add(slot, carry):
            term = coef_quintic * jnp.dot(
                gram[slot, j, :, body], ys[j], preferred_element_type=jnp.float32
            )
            for part in (PART_A, PART_B):
                place = place_of(slot, part)
                value = acc[place, :] + term[part[0] : part[0] + part[1], :]
                if last:
                    o_ref[place, :] = (factor * value).astype(jnp.bfloat16)
                else:
                    acc[place, :] = value
            return carry

        lax.fori_loop(0, 4, add, 0)

    def twice_mirrored():
        def add(slot, carry):
            acc[...] += coef_quintic * mirrored_terms(slot, ys)
            return carry

        lax.fori_loop(0, 4, add, 0)

    phase1(0, 0)
    phase1(0, 1)
    phase2(0, 0)
    phase2(0, 1)
    phase3(0)
    received([down_low])
    far_low = start(xs.at[1, low], xs.at[2, low], device(dz=-1))
    phase1(1, 0)
    received([up_high])
    far_high = start(xs.at[3, high], xs.at[2, high], device(dz=1))
    phase4(0)
    phase2(1, 0)
    phase5(0, 0)
    phase5(0, 1)
    received([down_high])
    phase1(1, 1)
    phase6(0, 0)
    phase6(0, 1)
    received([up_low])
    phase1(2, 0)
    phase1(2, 1)
    phase2(1, 1)
    phase3(1)
    phase2(2, 0)
    phase2(2, 1)
    phase4(1)
    phase3(2)
    received(shared[1])
    spread(3)
    phase4(2)
    phase5(3, 0)
    phase5(3, 1)
    received(shared[2])
    spread(2)
    phase6(3, 0)
    phase6(3, 1)
    phase5(1, 0)
    phase5(2, 0)
    phase5(1, 1)
    phase5(2, 1)
    received(step6[3])
    once_mirrored()
    received([far_low, far_high])
    received(step6[0])
    once("own", ((0, PART_A), (0, PART_B)))
    phase6(1, 0)
    phase6(2, 0)
    once("first", ((1, HALF_AA), (3, HALF_AA), (1, HALF_BA), (3, HALF_BA)))
    pass_on("own")
    phase6(1, 1)
    phase6(2, 1)
    once("second", ((1, HALF_AB), (3, HALF_AB), (1, HALF_BB), (3, HALF_BB)))
    pass_on("first")
    received(step6[1])
    received(step6[2])
    once("last", ((2, PART_A), (2, PART_B)))
    pass_on("second")
    twice(0)
    pass_on("last")
    twice_mirrored()
    twice(1)
    for name in ("own", "first", "second", "last"):
        received(forward[name])
    twice(2, last=True)
    sent(list(unsent))


def on_device(iterate):
    any_space = pl.BlockSpec(memory_space=pl.ANY)
    vmem = pl.BlockSpec(memory_space=pltpu.VMEM)
    bf16 = jnp.bfloat16
    return pl.pallas_call(
        kernel,
        out_shape=jax.ShapeDtypeStruct((BLOCK, DEPTH), bf16),
        in_specs=[any_space],
        out_specs=vmem,
        scratch_shapes=[
            pltpu.VMEM((4, BLOCK, DEPTH), bf16),
            pltpu.VMEM((2, 3, CHUNK, WIDE), bf16),
            pltpu.VMEM((2, CHUNK, FULL), bf16),
            pltpu.VMEM((2, CHUNK, WIDE), bf16),
            pltpu.VMEM((2, 2, CHUNK, WIDE), bf16),
            pltpu.VMEM((2, 3, CHUNK, PIECE), bf16),
            pltpu.VMEM((CHUNK, PIECE), bf16),
            pltpu.VMEM((4, 4, CHUNK, FULL), bf16),
            pltpu.VMEM((4, BLOCK, DEPTH), bf16),
            pltpu.VMEM((BLOCK, DEPTH), jnp.float32),
            pltpu.VMEM((352, DEPTH), jnp.float32),
            pltpu.SemaphoreType.DMA,
            pltpu.SemaphoreType.DMA((COPIES,)),
            pltpu.SemaphoreType.DMA((COPIES,)),
        ],
        compiler_params=pltpu.CompilerParams(
            collective_id=0, has_side_effects=True, vmem_limit_bytes=63 * 2**20
        ),
        name="newton_schulz",
    )(iterate)


def solution(mesh):
    return jax.shard_map(
        on_device,
        mesh=mesh,
        in_specs=(P(("layer", "row"), "col"),),
        out_specs=P(("layer", "row"), "col"),
        check_vma=False,
    )
```

```python
import functools
import math

import jax
import jax.numpy as jnp
from jax import lax
from jax.experimental import pallas as pl
from jax.experimental.pallas import tpu as pltpu
from jax.sharding import PartitionSpec as P

M = 5376
N = 12288

coef_linear = 3.4445
coef_cubic = -4.775
coef_quintic = 2.0315
factor = 0.2 * math.sqrt(max(M, N))

BLOCK = 1344
CHUNK = 336
SPLIT = 640
DEPTH = 768
WIDE = 1408
PIECE = 384
FULL = 4 * PIECE

PART_A = (0, 176)
PART_B = (176, 160)
HALF_AA = (0, 96)
HALF_AB = (96, 80)
HALF_BA = (176, 80)
HALF_BB = (256, 80)

TRANSPOSED = (((1,), (1,)), ((), ()))
LEFT_TRANSPOSED = (((0,), (0,)), ((), ()))
COPIES = 200


def rows_of(part):
    return pl.ds(part[0], part[1])


def kernel(
    x_hbm, o_ref, xs, send, summed, got_far, got_near, got_piece, handed, gram, ys, acc, y_acc,
    local_sem, send_sem, recv_sem,
):
    layer = lax.axis_index("layer")
    row = lax.axis_index("row")
    col = lax.axis_index("col")
    px = lax.div(col, 4)
    py = lax.rem(col, 4)
    pa = px * (1 - layer) + py * layer
    pb = py * (1 - layer) + px * layer

    def ring(position, step):
        return lax.rem(position + (step + 4), 4)

    def device(da=0, db=0, dz=0):
        na, nb = ring(pa, da), ring(pb, db)
        nx = na * (1 - layer) + nb * layer
        ny = nb * (1 - layer) + na * layer
        return (layer, ring(row, dz), nx * 4 + ny)

    used = [0]

    def start(src, dst, target):
        index = used[0]
        used[0] += 1
        copy = pltpu.make_async_remote_copy(
            src_ref=src,
            dst_ref=dst,
            send_sem=send_sem.at[index],
            recv_sem=recv_sem.at[index],
            device_id=target,
            device_id_type=pl.DeviceIdType.MESH,
        )
        copy.start()
        unsent.append(copy)
        return copy

    unsent = []

    def sent(copies):
        for copy in copies:
            copy.wait_send()
            unsent[:] = [other for other in unsent if other is not copy]

    landed = []

    def received(copies):
        for copy in copies:
            if not any(other is copy for other in landed):
                landed.append(copy)
                copy.wait_recv()

    partners = [device(dz=1), device(dz=-1)]
    for step in (1, 2, 3):
        partners += [device(da=step), device(db=step)]
    barrier = pltpu.get_barrier_semaphore()
    for partner in partners:
        pl.semaphore_signal(
            barrier, inc=1, device_id=partner, device_id_type=pl.DeviceIdType.MESH
        )
    own = pltpu.make_async_copy(x_hbm, xs.at[0], local_sem)
    own.start()
    pl.semaphore_wait(barrier, len(partners))

    low, high = pl.ds(0, SPLIT), pl.ds(SPLIT, BLOCK - SPLIT)
    down_low = start(x_hbm.at[low], xs.at[1, low], device(dz=-1))
    up_high = start(x_hbm.at[high], xs.at[3, high], device(dz=1))
    down_high = start(x_hbm.at[high], xs.at[1, high], device(dz=-1))
    up_low = start(x_hbm.at[low], xs.at[3, low], device(dz=1))

    for k in range(2):
        summed[k, :, pl.ds(1280, FULL - 1280)] = jnp.zeros((CHUNK, FULL - 1280), jnp.bfloat16)
    own.wait()

    def place_of(slot, part):
        position = pa if part[0] < PART_B[0] else pb
        return pl.ds(pl.multiple_of(ring(position, slot) * CHUNK + part[0], 16), part[1])

    def slot_rows(ref, j, slot):
        return jnp.concatenate(
            [ref[j, place_of(slot, PART_A), :], ref[j, place_of(slot, PART_B), :]], axis=0
        )

    def gram_terms(slot, j, columns):
        left, right = (3, 1) if j == 2 else (0, j)
        return lax.dot_general(
            slot_rows(xs, left, slot), xs[right, columns, :], TRANSPOSED,
            preferred_element_type=jnp.float32,
        )

    buffer_set = {0: 0, 1: 1, 2: 0}
    from_buffer = {}
    step1, step2, step3, step4, step5, step6 = {}, {}, {}, {}, {}, {}
    body = pl.ds(0, BLOCK)
    wide = pl.ds(0, WIDE)
    halves = (low, high)
    wide_halves = (low, pl.ds(SPLIT, WIDE - SPLIT))

    def reuse(name, j):
        key = name, buffer_set[j]
        owner, copies = from_buffer.get(key, (j, []))
        if owner != j:
            sent(copies)
            copies = []
        from_buffer[key] = (j, copies)
        return copies

    def phase1(j, h):
        k = buffer_set[j]
        copies = reuse("far", j)
        send[k, 0, :, halves[h]] = gram_terms(2, j, halves[h]).astype(jnp.bfloat16)
        step1[j, h] = []
        for half, target in (
            (HALF_AA, device(da=1)),
            (HALF_BA, device(db=1)),
            (HALF_AB, device(da=-1)),
            (HALF_BB, device(db=-1)),
        ):
            rows = rows_of(half)
            step1[j, h].append(
                start(
                    send.at[k, 0, rows, wide_halves[h]],
                    got_far.at[k, rows, wide_halves[h]],
                    target,
                )
            )
        copies += step1[j, h]

    def phase2(j, h):
        k = buffer_set[j]
        received(step1[j, h])
        step2[j, h] = []
        for side, slot, added in ((1, 1, (HALF_AA, HALF_BA)), (2, 3, (HALF_AB, HALF_BB))):
            copies = reuse(side, j)
            terms = gram_terms(slot, j, halves[h])
            for half in (HALF_AA, HALF_AB, HALF_BA, HALF_BB):
                rows = rows_of(half)
                value = terms[half[0] : half[0] + half[1], :]
                if half in added:
                    value = value + got_far[k, rows, halves[h]].astype(jnp.float32)
                send[k, side, rows, halves[h]] = value.astype(jnp.bfloat16)
            way = 1 if slot == 1 else -1
            for part, target in ((PART_A, device(da=way)), (PART_B, device(db=way))):
                rows = rows_of(part)
                copy = start(
                    send.at[k, side, rows, wide_halves[h]],
                    got_near.at[k, side - 1, rows, wide_halves[h]],
                    target,
                )
                copies.append(copy)
                step2[j, h].append(copy)

    def piece(position):
        return pl.ds(pl.multiple_of(position * PIECE, 128), PIECE)

    def phase3(j):
        k = buffer_set[j]
        copies = reuse("sum", j)
        for h in (0, 1):
            terms = gram_terms(0, j, halves[h])
            received(step2[j, h])
            summed[k, :, halves[h]] = (
                terms
                + got_near[k, 0, :, halves[h]].astype(jnp.float32)
                + got_near[k, 1, :, halves[h]].astype(jnp.float32)
            ).astype(jnp.bfloat16)
        step3[j] = []
        for step in (2, 1, 3):
            for part, place, target in (
                (PART_A, ring(pb, step), device(db=step)),
                (PART_B, ring(pa, step), device(da=step)),
            ):
                rows = rows_of(part)
                step3[j].append(
                    start(
                        summed.at[k, rows, piece(place)],
                        got_piece.at[k, step - 1, rows],
                        target,
                    )
                )
        copies += step3[j]

    def spread(j):
        step4[j] = []
        for step in (2, 1, 3):
            for part, place, target in (
                (PART_A, pb, device(db=step)),
                (PART_B, pa, device(da=step)),
            ):
                where = gram.at[0, j, rows_of(part), piece(place)]
                step4[j].append(start(where, where, target))

    def phase4(j):
        k = buffer_set[j]
        received(step3[j])
        for part, place in ((PART_A, pb), (PART_B, pa)):
            rows = rows_of(part)
            value = summed[k, rows, piece(place)].astype(jnp.float32)
            for step in range(3):
                value = value + got_piece[k, step, rows, :].astype(jnp.float32)
            value = value.astype(jnp.bfloat16)
            if j == 2:
                handed[rows, :] = value
            else:
                gram[0, j, rows, piece(place)] = value
        if j != 0:
            shared[j] = []
            for part, place in ((PART_A, pb), (PART_B, pa)):
                rows = rows_of(part)
                if j == 1:
                    src, theirs, way = gram.at[0, 1, rows, piece(place)], 3, 1
                else:
                    src, theirs, way = handed.at[rows], 2, -1
                shared[j].append(
                    start(src, gram.at[0, theirs, rows, piece(place)], device(dz=way))
                )
        if j != 2:
            spread(j)

    shared = {}

    def phase5(j, half):
        if half == 0:
            received(step4[j])
            step5[j] = []
        copies = []
        for rows_half, target_up, target_down in (
            ((HALF_AA, HALF_AB)[half], device(da=1), device(da=-1)),
            ((HALF_BA, HALF_BB)[half], device(db=1), device(db=-1)),
        ):
            rows = rows_of(rows_half)
            src = gram.at[0, j, rows, wide]
            copies.append(start(src, gram.at[3, j, rows, wide], target_up))
            copies.append(start(src, gram.at[1, j, rows, wide], target_down))
        step5[j].append(copies)

    def phase6(j, half):
        received(step5[j][half])
        if half == 0:
            step6[j] = []
        for rows_half, target in (
            ((HALF_AA, HALF_AB)[half], device(da=(1, -1)[half])),
            ((HALF_BA, HALF_BB)[half], device(db=(1, -1)[half])),
        ):
            rows = rows_of(rows_half)
            step6[j].append(
                start(
                    gram.at[(3, 1)[half], j, rows, wide], gram.at[2, j, rows, wide], target
                )
            )

    direct, forward = {}, {}

    def mirrored_terms(slot, ref):
        return lax.dot_general(
            gram[slot, 3, :, body], slot_rows(ref, 3, slot), LEFT_TRANSPOSED,
            preferred_element_type=jnp.float32,
        )

    def once_mirrored(slot, first=False):
        terms = mirrored_terms(slot, xs)
        acc[...] = terms if first else acc[...] + terms

    def once_add(j, pieces):
        left = [gram[slot, j, rows_of(part), body] for slot, part in pieces]
        left = left[0] if len(left) == 1 else jnp.concatenate(left, axis=0)
        term = jnp.dot(left, xs[j], preferred_element_type=jnp.float32)
        rows = pl.ds(0, sum(part[1] for _, part in pieces))
        y_acc[rows, :] = term if j == 0 else y_acc[rows, :] + term

    def once(name, pieces):
        offset = 0
        for slot, part in pieces:
            place = place_of(slot, part)
            value = y_acc[pl.ds(offset, part[1]), :] + acc[place, :]
            offset += part[1]
            acc[place, :] = coef_linear * xs[0, place, :].astype(jnp.float32) + coef_cubic * value
            ys[0, place, :] = value.astype(jnp.bfloat16)
        direct[name] = []
        for slot, part in pieces:
            place = place_of(slot, part)
            src = ys.at[0, place]
            direct[name].append(
                (
                    slot,
                    part,
                    start(src, ys.at[3, place], device(dz=1)),
                    start(src, ys.at[1, place], device(dz=-1)),
                )
            )

    def pass_on(name):
        forward[name] = []
        for slot, part, up, down in direct[name]:
            place = place_of(slot, part)
            received([up, down])
            if part[0] < PART_B[0]:
                copy = start(ys.at[3, place], ys.at[2, place], device(dz=1))
            else:
                copy = start(ys.at[1, place], ys.at[2, place], device(dz=-1))
            forward[name].append(copy)

    def twice(j, last=False):
        def add(slot, carry):
            term = coef_quintic * jnp.dot(
                gram[slot, j, :, body], ys[j], preferred_element_type=jnp.float32
            )
            for part in (PART_A, PART_B):
                place = place_of(slot, part)
                value = acc[place, :] + term[part[0] : part[0] + part[1], :]
                if last:
                    o_ref[place, :] = (factor * value).astype(jnp.bfloat16)
                else:
                    acc[place, :] = value
            return carry

        lax.fori_loop(0, 4, add, 0)

    def twice_mirrored():
        def add(slot, carry):
            acc[...] += coef_quintic * mirrored_terms(slot, ys)
            return carry

        lax.fori_loop(0, 4, add, 0)

    slot_own = ((0, PART_A), (0, PART_B))
    slot_first = ((1, HALF_AA), (3, HALF_AA), (1, HALF_BA), (3, HALF_BA))
    slot_second = ((1, HALF_AB), (3, HALF_AB), (1, HALF_BB), (3, HALF_BB))
    slot_last = ((2, PART_A), (2, PART_B))

    phase1(0, 0)
    phase1(0, 1)
    phase2(0, 0)
    phase2(0, 1)
    phase3(0)
    received([down_low])
    far_low = start(xs.at[1, low], xs.at[2, low], device(dz=-1))
    phase1(1, 0)
    received([up_high])
    far_high = start(xs.at[3, high], xs.at[2, high], device(dz=1))
    phase4(0)
    phase2(1, 0)
    received([down_high])
    phase1(1, 1)
    received([up_low])
    phase1(2, 0)
    phase1(2, 1)
    phase2(1, 1)
    phase3(1)
    phase2(2, 0)
    phase2(2, 1)
    phase4(1)
    received(step4[0])
    phase3(2)
    received(shared[1])
    spread(3)
    phase4(2)
    phase5(3, 0)
    phase5(3, 1)
    once_add(0, slot_own)
    once_mirrored(0, first=True)
    received(shared[2])
    spread(2)
    phase6(3, 0)
    phase6(3, 1)
    received(step4[1])
    once_add(1, slot_own)
    phase5(0, 0)
    phase5(1, 0)
    once_mirrored(1)
    once_mirrored(3)
    phase5(2, 0)
    received([far_low, far_high])
    once_add(2, slot_own)
    phase5(0, 1)
    phase5(1, 1)
    phase5(2, 1)
    received(step6[3])
    once_mirrored(2)
    once("own", slot_own)
    for j in range(3):
        phase6(j, 0)
        once_add(j, slot_first)
    once("first", slot_first)
    pass_on("own")
    for j in range(3):
        phase6(j, 1)
        once_add(j, slot_second)
    once("second", slot_second)
    pass_on("first")
    for j in range(3):
        received(step6[j])
        once_add(j, slot_last)
    once("last", slot_last)
    pass_on("second")
    twice(0)
    pass_on("last")
    twice_mirrored()
    twice(1)
    for name in ("own", "first", "second", "last"):
        received(forward[name])
    twice(2, last=True)
    sent(list(unsent))


def on_device(iterate):
    any_space = pl.BlockSpec(memory_space=pl.ANY)
    vmem = pl.BlockSpec(memory_space=pltpu.VMEM)
    bf16 = jnp.bfloat16
    return pl.pallas_call(
        kernel,
        out_shape=jax.ShapeDtypeStruct((BLOCK, DEPTH), bf16),
        in_specs=[any_space],
        out_specs=vmem,
        scratch_shapes=[
            pltpu.VMEM((4, BLOCK, DEPTH), bf16),
            pltpu.VMEM((2, 3, CHUNK, WIDE), bf16),
            pltpu.VMEM((2, CHUNK, FULL), bf16),
            pltpu.VMEM((2, CHUNK, WIDE), bf16),
            pltpu.VMEM((2, 2, CHUNK, WIDE), bf16),
            pltpu.VMEM((2, 3, CHUNK, PIECE), bf16),
            pltpu.VMEM((CHUNK, PIECE), bf16),
            pltpu.VMEM((4, 4, CHUNK, FULL), bf16),
            pltpu.VMEM((4, BLOCK, DEPTH), bf16),
            pltpu.VMEM((BLOCK, DEPTH), jnp.float32),
            pltpu.VMEM((352, DEPTH), jnp.float32),
            pltpu.SemaphoreType.DMA,
            pltpu.SemaphoreType.DMA((COPIES,)),
            pltpu.SemaphoreType.DMA((COPIES,)),
        ],
        compiler_params=pltpu.CompilerParams(
            collective_id=0, has_side_effects=True, vmem_limit_bytes=63 * 2**20
        ),
        name="newton_schulz",
    )(iterate)


def solution(mesh):
    return jax.shard_map(
        on_device,
        mesh=mesh,
        in_specs=(P(("layer", "row"), "col"),),
        out_specs=P(("layer", "row"), "col"),
        check_vma=False,
    )
```

```python
import functools
import math

import jax
import jax.numpy as jnp
from jax import lax
from jax.experimental import pallas as pl
from jax.experimental.pallas import tpu as pltpu
from jax.sharding import PartitionSpec as P

M = 5376
N = 12288

coef_linear = 3.4445
coef_cubic = -4.775
coef_quintic = 2.0315
factor = 0.2 * math.sqrt(max(M, N))

BLOCK = 1344
CHUNK = 336
THIRDS = ((0, 512, 512), (512, 512, 512), (1024, 320, 384))
DEPTH = 768
WIDE = 1408
PIECE = 384
FULL = 4 * PIECE

PART_A = (0, 176)
PART_B = (176, 160)
HALF_AA = (0, 96)
HALF_AB = (96, 80)
HALF_BA = (176, 80)
HALF_BB = (256, 80)

TRANSPOSED = (((1,), (1,)), ((), ()))
LEFT_TRANSPOSED = (((0,), (0,)), ((), ()))
COPIES = 230


def rows_of(part):
    return pl.ds(part[0], part[1])


def kernel(
    x_hbm, o_ref, xs, send, summed, got_far, got_near, got_piece, handed, gram, ys, acc, y_acc,
    local_sem, send_sem, recv_sem,
):
    layer = lax.axis_index("layer")
    row = lax.axis_index("row")
    col = lax.axis_index("col")
    px = lax.div(col, 4)
    py = lax.rem(col, 4)
    pa = px * (1 - layer) + py * layer
    pb = py * (1 - layer) + px * layer

    def ring(position, step):
        return lax.rem(position + (step + 4), 4)

    def device(da=0, db=0, dz=0):
        na, nb = ring(pa, da), ring(pb, db)
        nx = na * (1 - layer) + nb * layer
        ny = nb * (1 - layer) + na * layer
        return (layer, ring(row, dz), nx * 4 + ny)

    used = [0]

    def start(src, dst, target):
        index = used[0]
        used[0] += 1
        copy = pltpu.make_async_remote_copy(
            src_ref=src,
            dst_ref=dst,
            send_sem=send_sem.at[index],
            recv_sem=recv_sem.at[index],
            device_id=target,
            device_id_type=pl.DeviceIdType.MESH,
        )
        copy.start()
        unsent.append(copy)
        return copy

    unsent = []

    def sent(copies):
        for copy in copies:
            copy.wait_send()
            unsent[:] = [other for other in unsent if other is not copy]

    landed = []

    def received(copies):
        for copy in copies:
            if not any(other is copy for other in landed):
                landed.append(copy)
                copy.wait_recv()

    partners = [device(dz=1), device(dz=-1)]
    for step in (1, 2, 3):
        partners += [device(da=step), device(db=step)]
    barrier = pltpu.get_barrier_semaphore()
    for partner in partners:
        pl.semaphore_signal(
            barrier, inc=1, device_id=partner, device_id_type=pl.DeviceIdType.MESH
        )
    own = pltpu.make_async_copy(x_hbm, xs.at[0], local_sem)
    own.start()
    pl.semaphore_wait(barrier, len(partners))

    def place_of(slot, part):
        position = pa if part[0] < PART_B[0] else pb
        return pl.ds(pl.multiple_of(ring(position, slot) * CHUNK + part[0], 16), part[1])

    columns = [pl.ds(first, count) for first, count, _ in THIRDS]
    wide_columns = [pl.ds(first, count) for first, _, count in THIRDS]
    from_next, from_last = {}, {}

    def send_down(h):
        from_next[h] = [start(x_hbm.at[columns[h]], xs.at[1, columns[h]], device(dz=-1))]

    def send_up(slot):
        from_last[slot] = []
        for part in (PART_A, PART_B):
            place = place_of(slot, part)
            from_last[slot].append(start(x_hbm.at[place], xs.at[3, place], device(dz=1)))

    send_down(0)
    send_up(2)
    send_down(1)
    send_up(1)
    send_up(3)
    send_down(2)
    send_up(0)

    for k in range(2):
        summed[k, :, pl.ds(1280, FULL - 1280)] = jnp.zeros((CHUNK, FULL - 1280), jnp.bfloat16)
    own.wait()

    far = []

    def send_far(j, slot):
        for part in (PART_A, PART_B):
            place = place_of(slot, part)
            way = device(dz=1) if j == 3 else device(dz=-1)
            far.append(start(xs.at[j, place], xs.at[2, place], way))

    def slot_rows(ref, j, slot):
        return jnp.concatenate(
            [ref[j, place_of(slot, PART_A), :], ref[j, place_of(slot, PART_B), :]], axis=0
        )

    def gram_terms(slot, j, h):
        left, right = (3, 1) if j == 2 else (0, j)
        return lax.dot_general(
            slot_rows(xs, left, slot), xs[right, columns[h], :], TRANSPOSED,
            preferred_element_type=jnp.float32,
        )

    buffer_set = {0: 0, 1: 1, 2: 0}
    from_buffer = {}
    step1, step2, step3, step4, step5, step6 = {}, {}, {}, {}, {}, {}
    body = pl.ds(0, BLOCK)
    wide = pl.ds(0, WIDE)

    def reuse(name, j):
        key = name, buffer_set[j]
        owner, copies = from_buffer.get(key, (j, []))
        if owner != j:
            sent(copies)
            copies = []
        from_buffer[key] = (j, copies)
        return copies

    def phase1(j, h):
        k = buffer_set[j]
        copies = reuse("far", j)
        send[k, 0, :, columns[h]] = gram_terms(2, j, h).astype(jnp.bfloat16)
        step1[j, h] = []
        for half, target in (
            (HALF_AA, device(da=1)),
            (HALF_BA, device(db=1)),
            (HALF_AB, device(da=-1)),
            (HALF_BB, device(db=-1)),
        ):
            rows = rows_of(half)
            step1[j, h].append(
                start(
                    send.at[k, 0, rows, wide_columns[h]],
                    got_far.at[k, rows, wide_columns[h]],
                    target,
                )
            )
        copies += step1[j, h]

    def phase2(j, h):
        k = buffer_set[j]
        received(step1[j, h])
        step2[j, h] = []
        for side, slot, added in ((1, 1, (HALF_AA, HALF_BA)), (2, 3, (HALF_AB, HALF_BB))):
            copies = reuse(side, j)
            terms = gram_terms(slot, j, h)
            for half in (HALF_AA, HALF_AB, HALF_BA, HALF_BB):
                rows = rows_of(half)
                value = terms[half[0] : half[0] + half[1], :]
                if half in added:
                    value = value + got_far[k, rows, columns[h]].astype(jnp.float32)
                send[k, side, rows, columns[h]] = value.astype(jnp.bfloat16)
            way = 1 if slot == 1 else -1
            for part, target in ((PART_A, device(da=way)), (PART_B, device(db=way))):
                rows = rows_of(part)
                copy = start(
                    send.at[k, side, rows, wide_columns[h]],
                    got_near.at[k, side - 1, rows, wide_columns[h]],
                    target,
                )
                copies.append(copy)
                step2[j, h].append(copy)

    def piece(position):
        return pl.ds(pl.multiple_of(position * PIECE, 128), PIECE)

    def phase3(j):
        k = buffer_set[j]
        copies = reuse("sum", j)
        for h in range(3):
            terms = gram_terms(0, j, h)
            received(step2[j, h])
            summed[k, :, columns[h]] = (
                terms
                + got_near[k, 0, :, columns[h]].astype(jnp.float32)
                + got_near[k, 1, :, columns[h]].astype(jnp.float32)
            ).astype(jnp.bfloat16)
        step3[j] = []
        for step in (2, 1, 3):
            for part, place, target in (
                (PART_A, ring(pb, step), device(db=step)),
                (PART_B, ring(pa, step), device(da=step)),
            ):
                rows = rows_of(part)
                step3[j].append(
                    start(
                        summed.at[k, rows, piece(place)],
                        got_piece.at[k, step - 1, rows],
                        target,
                    )
                )
        copies += step3[j]

    def spread(j):
        step4[j] = []
        for step in (2, 1, 3):
            for part, place, target in (
                (PART_A, pb, device(db=step)),
                (PART_B, pa, device(da=step)),
            ):
                where = gram.at[0, j, rows_of(part), piece(place)]
                step4[j].append(start(where, where, target))

    def phase4(j):
        k = buffer_set[j]
        received(step3[j])
        for part, place in ((PART_A, pb), (PART_B, pa)):
            rows = rows_of(part)
            value = summed[k, rows, piece(place)].astype(jnp.float32)
            for step in range(3):
                value = value + got_piece[k, step, rows, :].astype(jnp.float32)
            value = value.astype(jnp.bfloat16)
            if j == 2:
                handed[rows, :] = value
            else:
                gram[0, j, rows, piece(place)] = value
        if j != 0:
            shared[j] = []
            for part, place in ((PART_A, pb), (PART_B, pa)):
                rows = rows_of(part)
                if j == 1:
                    src, theirs, way = gram.at[0, 1, rows, piece(place)], 3, 1
                else:
                    src, theirs, way = handed.at[rows], 2, -1
                shared[j].append(
                    start(src, gram.at[0, theirs, rows, piece(place)], device(dz=way))
                )
        if j != 2:
            spread(j)

    shared = {}

    def phase5(j, half):
        if half == 0:
            received(step4[j])
            step5[j] = []
        copies = []
        for rows_half, target_up, target_down in (
            ((HALF_AA, HALF_AB)[half], device(da=1), device(da=-1)),
            ((HALF_BA, HALF_BB)[half], device(db=1), device(db=-1)),
        ):
            rows = rows_of(rows_half)
            src = gram.at[0, j, rows, wide]
            copies.append(start(src, gram.at[3, j, rows, wide], target_up))
            copies.append(start(src, gram.at[1, j, rows, wide], target_down))
        step5[j].append(copies)

    def phase6(j, half):
        received(step5[j][half])
        if half == 0:
            step6[j] = []
        for rows_half, target in (
            ((HALF_AA, HALF_AB)[half], device(da=(1, -1)[half])),
            ((HALF_BA, HALF_BB)[half], device(db=(1, -1)[half])),
        ):
            rows = rows_of(rows_half)
            step6[j].append(
                start(
                    gram.at[(3, 1)[half], j, rows, wide], gram.at[2, j, rows, wide], target
                )
            )

    direct, forward = {}, {}

    def mirrored_terms(slot, ref):
        return lax.dot_general(
            gram[slot, 3, :, body], slot_rows(ref, 3, slot), LEFT_TRANSPOSED,
            preferred_element_type=jnp.float32,
        )

    def once_mirrored(slot, first=False):
        terms = mirrored_terms(slot, xs)
        acc[...] = terms if first else acc[...] + terms

    def once_add(j, pieces):
        left = [gram[slot, j, rows_of(part), body] for slot, part in pieces]
        left = left[0] if len(left) == 1 else jnp.concatenate(left, axis=0)
        term = jnp.dot(left, xs[j], preferred_element_type=jnp.float32)
        rows = pl.ds(0, sum(part[1] for _, part in pieces))
        y_acc[rows, :] = term if j == 0 else y_acc[rows, :] + term

    def once(name, pieces):
        offset = 0
        for slot, part in pieces:
            place = place_of(slot, part)
            value = y_acc[pl.ds(offset, part[1]), :] + acc[place, :]
            offset += part[1]
            acc[place, :] = coef_linear * xs[0, place, :].astype(jnp.float32) + coef_cubic * value
            ys[0, place, :] = value.astype(jnp.bfloat16)
        first = [p for p in pieces if p[1][0] < PART_B[0]]
        second = [p for p in pieces if p[1][0] >= PART_B[0]]
        direct[name] = {}
        for ups, downs in ((first, second), (second, first)):
            for way, block, group in ((1, 3, ups), (-1, 1, downs)):
                for slot, part in group:
                    place = place_of(slot, part)
                    direct[name][way, slot, part] = start(
                        ys.at[0, place], ys.at[block, place], device(dz=way)
                    )

    def pass_on(name):
        forward[name] = []
        for (way, slot, part), copy in direct[name].items():
            if (part[0] < PART_B[0]) == (way == 1):
                received([copy])
                place = place_of(slot, part)
                block = 3 if way == 1 else 1
                forward[name].append(
                    start(ys.at[block, place], ys.at[2, place], device(dz=way))
                )

    def twice(j, last=False):
        def add(slot, carry):
            term = coef_quintic * jnp.dot(
                gram[slot, j, :, body], ys[j], preferred_element_type=jnp.float32
            )
            for part in (PART_A, PART_B):
                place = place_of(slot, part)
                value = acc[place, :] + term[part[0] : part[0] + part[1], :]
                if last:
                    o_ref[place, :] = (factor * value).astype(jnp.bfloat16)
                else:
                    acc[place, :] = value
            return carry

        lax.fori_loop(0, 4, add, 0)

    def twice_mirrored(slot):
        acc[...] += coef_quintic * mirrored_terms(slot, ys)

    slot_own = ((0, PART_A), (0, PART_B))
    slot_first = ((1, HALF_AA), (3, HALF_AA), (1, HALF_BA), (3, HALF_BA))
    slot_second = ((1, HALF_AB), (3, HALF_AB), (1, HALF_BB), (3, HALF_BB))
    slot_last = ((2, PART_A), (2, PART_B))

    for h in range(3):
        phase1(0, h)
    for h in range(3):
        phase2(0, h)
    phase3(0)
    received(from_next[0])
    phase1(1, 0)
    phase4(0)
    received(from_last[2])
    phase1(2, 0)
    phase2(1, 0)
    received(from_next[1])
    phase1(1, 1)
    received(from_last[1])
    received(from_last[3])
    send_far(3, 2)
    send_far(3, 1)
    phase2(2, 0)
    phase1(2, 1)
    phase2(1, 1)
    phase2(2, 1)
    received(from_next[2])
    phase1(1, 2)
    send_far(1, 3)
    send_far(1, 0)
    phase1(2, 2)
    phase2(1, 2)
    phase3(1)
    received(from_last[0])
    phase2(2, 2)
    phase4(1)
    received(step4[0])
    phase3(2)
    received(shared[1])
    spread(3)
    phase4(2)
    phase5(3, 0)
    phase5(3, 1)
    once_add(0, slot_own)
    once_mirrored(0, first=True)
    received(shared[2])
    spread(2)
    phase6(3, 0)
    phase6(3, 1)
    received(step4[1])
    once_add(1, slot_own)
    phase5(0, 0)
    phase5(1, 0)
    once_mirrored(1)
    once_mirrored(3)
    phase5(2, 0)
    received(far)
    once_add(2, slot_own)
    phase5(0, 1)
    phase5(1, 1)
    phase5(2, 1)
    received(step6[3])
    once_mirrored(2)
    once("own", slot_own)
    for j in range(3):
        phase6(j, 0)
        once_add(j, slot_first)
    once("first", slot_first)
    pass_on("own")
    for j in range(3):
        phase6(j, 1)
        once_add(j, slot_second)
    once("second", slot_second)
    pass_on("first")
    for j in range(3):
        received(step6[j])
        once_add(j, slot_last)
    once("last", slot_last)
    pass_on("second")
    twice(0)
    for name in ("own", "first", "second"):
        received(direct[name].values())
    twice_mirrored(0)
    twice_mirrored(1)
    twice_mirrored(3)
    pass_on("last")
    received(direct["last"].values())
    twice_mirrored(2)
    twice(1)
    for name in ("own", "first", "second", "last"):
        received(forward[name])
    twice(2, last=True)
    sent(list(unsent))


def on_device(iterate):
    any_space = pl.BlockSpec(memory_space=pl.ANY)
    vmem = pl.BlockSpec(memory_space=pltpu.VMEM)
    bf16 = jnp.bfloat16
    return pl.pallas_call(
        kernel,
        out_shape=jax.ShapeDtypeStruct((BLOCK, DEPTH), bf16),
        in_specs=[any_space],
        out_specs=vmem,
        scratch_shapes=[
            pltpu.VMEM((4, BLOCK, DEPTH), bf16),
            pltpu.VMEM((2, 3, CHUNK, WIDE), bf16),
            pltpu.VMEM((2, CHUNK, FULL), bf16),
            pltpu.VMEM((2, CHUNK, WIDE), bf16),
            pltpu.VMEM((2, 2, CHUNK, WIDE), bf16),
            pltpu.VMEM((2, 3, CHUNK, PIECE), bf16),
            pltpu.VMEM((CHUNK, PIECE), bf16),
            pltpu.VMEM((4, 4, CHUNK, FULL), bf16),
            pltpu.VMEM((4, BLOCK, DEPTH), bf16),
            pltpu.VMEM((BLOCK, DEPTH), jnp.float32),
            pltpu.VMEM((352, DEPTH), jnp.float32),
            pltpu.SemaphoreType.DMA,
            pltpu.SemaphoreType.DMA((COPIES,)),
            pltpu.SemaphoreType.DMA((COPIES,)),
        ],
        compiler_params=pltpu.CompilerParams(
            collective_id=0, has_side_effects=True, vmem_limit_bytes=63 * 2**20
        ),
        name="newton_schulz",
    )(iterate)


def solution(mesh):
    return jax.shard_map(
        on_device,
        mesh=mesh,
        in_specs=(P(("layer", "row"), "col"),),
        out_specs=P(("layer", "row"), "col"),
        check_vma=False,
    )
```

```python
import functools
import math

import jax
import jax.numpy as jnp
from jax import lax
from jax.experimental import pallas as pl
from jax.experimental.pallas import tpu as pltpu
from jax.sharding import PartitionSpec as P

M = 5376
N = 12288

coef_linear = 3.4445
coef_cubic = -4.775
coef_quintic = 2.0315
factor = 0.2 * math.sqrt(max(M, N))

BLOCK = 1344
CHUNK = 336
THIRDS = ((0, 512, 512), (512, 512, 512), (1024, 320, 384))
DEPTH = 768
WIDE = 1408
PIECE = 384
FULL = 4 * PIECE

PART_A = (0, 176)
PART_B = (176, 160)
HALF_AA = (0, 96)
HALF_AB = (96, 80)
HALF_BA = (176, 80)
HALF_BB = (256, 80)

TRANSPOSED = (((1,), (1,)), ((), ()))
LEFT_TRANSPOSED = (((0,), (0,)), ((), ()))
COPIES = 250


def rows_of(part):
    return pl.ds(part[0], part[1])


def kernel(
    x_hbm, o_ref, xs, send, summed, got_far, got_near, relayed, got_piece, handed, gram, ys, acc,
    y_acc,
    local_sem, send_sem, recv_sem,
):
    layer = lax.axis_index("layer")
    row = lax.axis_index("row")
    col = lax.axis_index("col")
    px = lax.div(col, 4)
    py = lax.rem(col, 4)
    pa = px * (1 - layer) + py * layer
    pb = py * (1 - layer) + px * layer

    def ring(position, step):
        return lax.rem(position + (step + 4), 4)

    def device(da=0, db=0, dz=0):
        na, nb = ring(pa, da), ring(pb, db)
        nx = na * (1 - layer) + nb * layer
        ny = nb * (1 - layer) + na * layer
        return (layer, ring(row, dz), nx * 4 + ny)

    used = [0]

    def start(src, dst, target):
        index = used[0]
        used[0] += 1
        copy = pltpu.make_async_remote_copy(
            src_ref=src,
            dst_ref=dst,
            send_sem=send_sem.at[index],
            recv_sem=recv_sem.at[index],
            device_id=target,
            device_id_type=pl.DeviceIdType.MESH,
        )
        copy.start()
        unsent.append(copy)
        return copy

    unsent = []

    def sent(copies):
        for copy in copies:
            copy.wait_send()
            unsent[:] = [other for other in unsent if other is not copy]

    landed = []

    def received(copies):
        for copy in copies:
            if not any(other is copy for other in landed):
                landed.append(copy)
                copy.wait_recv()

    partners = [device(dz=1), device(dz=-1)]
    for step in (1, 2, 3):
        partners += [device(da=step), device(db=step)]
    barrier = pltpu.get_barrier_semaphore()
    for partner in partners:
        pl.semaphore_signal(
            barrier, inc=1, device_id=partner, device_id_type=pl.DeviceIdType.MESH
        )
    own = pltpu.make_async_copy(x_hbm, xs.at[0], local_sem)
    own.start()
    pl.semaphore_wait(barrier, len(partners))

    def place_of(slot, part):
        position = pa if part[0] < PART_B[0] else pb
        return pl.ds(pl.multiple_of(ring(position, slot) * CHUNK + part[0], 16), part[1])

    columns = [pl.ds(first, count) for first, count, _ in THIRDS]
    wide_columns = [pl.ds(first, count) for first, _, count in THIRDS]
    from_next, from_last = {}, {}

    def send_down(h):
        from_next[h] = [start(x_hbm.at[columns[h]], xs.at[1, columns[h]], device(dz=-1))]

    def send_up(slot):
        from_last[slot] = []
        for part in (PART_A, PART_B):
            place = place_of(slot, part)
            from_last[slot].append(start(x_hbm.at[place], xs.at[3, place], device(dz=1)))

    send_down(0)
    send_up(2)
    send_down(1)
    send_up(1)
    send_up(3)
    send_down(2)
    send_up(0)

    for k in range(2):
        summed[k, :, pl.ds(1280, FULL - 1280)] = jnp.zeros((CHUNK, FULL - 1280), jnp.bfloat16)
    own.wait()

    far = []

    def send_far(j, slot):
        for part in (PART_A, PART_B):
            place = place_of(slot, part)
            way = device(dz=1) if j == 3 else device(dz=-1)
            far.append(start(xs.at[j, place], xs.at[2, place], way))

    def slot_rows(ref, j, slot):
        return jnp.concatenate(
            [ref[j, place_of(slot, PART_A), :], ref[j, place_of(slot, PART_B), :]], axis=0
        )

    def gram_terms(slot, j, h):
        left, right = (3, 1) if j == 2 else (0, j)
        return lax.dot_general(
            slot_rows(xs, left, slot), xs[right, columns[h], :], TRANSPOSED,
            preferred_element_type=jnp.float32,
        )

    buffer_set = {0: 0, 1: 1, 2: 0}
    from_buffer = {}
    step1, step2, step3, step3_on = {}, {}, {}, {}
    step4, step4_on, step5, step6 = {}, {}, {}, {}
    second_rings = (
        ((HALF_AA, HALF_AB), pb, lambda way: device(db=way)),
        ((HALF_BA, HALF_BB), pa, lambda way: device(da=way)),
    )
    body = pl.ds(0, BLOCK)
    wide = pl.ds(0, WIDE)

    def reuse(name, j):
        key = name, buffer_set[j]
        owner, copies = from_buffer.get(key, (j, []))
        if owner != j:
            sent(copies)
            copies = []
        from_buffer[key] = (j, copies)
        return copies

    def phase1(j, h):
        k = buffer_set[j]
        copies = reuse("far", j)
        send[k, 0, :, columns[h]] = gram_terms(2, j, h).astype(jnp.bfloat16)
        step1[j, h] = []
        for half, target in (
            (HALF_AA, device(da=1)),
            (HALF_BA, device(db=1)),
            (HALF_AB, device(da=-1)),
            (HALF_BB, device(db=-1)),
        ):
            rows = rows_of(half)
            step1[j, h].append(
                start(
                    send.at[k, 0, rows, wide_columns[h]],
                    got_far.at[k, rows, wide_columns[h]],
                    target,
                )
            )
        copies += step1[j, h]

    def phase2(j, h):
        k = buffer_set[j]
        received(step1[j, h])
        step2[j, h] = []
        for side, slot, added in ((1, 1, (HALF_AA, HALF_BA)), (2, 3, (HALF_AB, HALF_BB))):
            copies = reuse(side, j)
            terms = gram_terms(slot, j, h)
            for half in (HALF_AA, HALF_AB, HALF_BA, HALF_BB):
                rows = rows_of(half)
                value = terms[half[0] : half[0] + half[1], :]
                if half in added:
                    value = value + got_far[k, rows, columns[h]].astype(jnp.float32)
                send[k, side, rows, columns[h]] = value.astype(jnp.bfloat16)
            way = 1 if slot == 1 else -1
            for part, target in ((PART_A, device(da=way)), (PART_B, device(db=way))):
                rows = rows_of(part)
                copy = start(
                    send.at[k, side, rows, wide_columns[h]],
                    got_near.at[k, side - 1, rows, wide_columns[h]],
                    target,
                )
                copies.append(copy)
                step2[j, h].append(copy)

    def piece(position):
        return pl.ds(pl.multiple_of(position * PIECE, 128), PIECE)

    def phase3(j):
        k = buffer_set[j]
        copies = reuse("sum", j)
        for h in range(3):
            terms = gram_terms(0, j, h)
            received(step2[j, h])
            summed[k, :, columns[h]] = (
                terms
                + got_near[k, 0, :, columns[h]].astype(jnp.float32)
                + got_near[k, 1, :, columns[h]].astype(jnp.float32)
            ).astype(jnp.bfloat16)
        step3[j] = []
        for halves, position, ring_device in second_rings:
            place = piece(ring(position, 2))
            for half, way in zip(halves, (1, -1)):
                rows = rows_of(half)
                step3[j].append(
                    start(summed.at[k, rows, place], relayed.at[k, rows], ring_device(way))
                )
        copies += step3[j]

    def phase3_on(j):
        k = buffer_set[j]
        received(step3[j])
        step3_on[j] = []
        for (_, position, ring_device), part in zip(second_rings, (PART_A, PART_B)):
            for side, way in enumerate((1, -1)):
                place = piece(ring(position, way))
                half = second_rings[part == PART_B][0][side]
                rows = rows_of(half)
                summed[k, rows, place] = (
                    summed[k, rows, place].astype(jnp.float32)
                    + relayed[k, rows, :].astype(jnp.float32)
                ).astype(jnp.bfloat16)
                rows = rows_of(part)
                step3_on[j].append(
                    start(
                        summed.at[k, rows, place], got_piece.at[k, side, rows], ring_device(way)
                    )
                )
        from_buffer["sum", k][1].extend(step3_on[j])

    def spread(j):
        step4[j] = []
        for (_, position, ring_device), part in zip(second_rings, (PART_A, PART_B)):
            where = gram.at[0, j, rows_of(part), piece(position)]
            for way in (1, -1):
                step4[j].append(start(where, where, ring_device(way)))

    def spread_on(j):
        received(step4[j])
        step4_on[j] = []
        for halves, position, ring_device in second_rings:
            for half, way in zip(halves, (1, -1)):
                where = gram.at[0, j, rows_of(half), piece(ring(position, -way))]
                step4_on[j].append(start(where, where, ring_device(way)))

    def phase4(j):
        k = buffer_set[j]
        received(step3_on[j])
        for part, place in ((PART_A, pb), (PART_B, pa)):
            rows = rows_of(part)
            value = summed[k, rows, piece(place)].astype(jnp.float32)
            for side in range(2):
                value = value + got_piece[k, side, rows, :].astype(jnp.float32)
            value = value.astype(jnp.bfloat16)
            if j == 2:
                handed[rows, :] = value
            else:
                gram[0, j, rows, piece(place)] = value
        if j != 0:
            shared[j] = []
            for part, place in ((PART_A, pb), (PART_B, pa)):
                rows = rows_of(part)
                if j == 1:
                    src, theirs, way = gram.at[0, 1, rows, piece(place)], 3, 1
                else:
                    src, theirs, way = handed.at[rows], 2, -1
                shared[j].append(
                    start(src, gram.at[0, theirs, rows, piece(place)], device(dz=way))
                )
        if j == 0:
            spread(j)

    shared = {}

    def phase5(j, half):
        if half == 0:
            received(step4_on[j])
            step5[j] = []
        copies = []
        for rows_half, target_up, target_down in (
            ((HALF_AA, HALF_AB)[half], device(da=1), device(da=-1)),
            ((HALF_BA, HALF_BB)[half], device(db=1), device(db=-1)),
        ):
            rows = rows_of(rows_half)
            src = gram.at[0, j, rows, wide]
            copies.append(start(src, gram.at[3, j, rows, wide], target_up))
            copies.append(start(src, gram.at[1, j, rows, wide], target_down))
        step5[j].append(copies)

    def phase6(j, half):
        received(step5[j][half])
        if half == 0:
            step6[j] = []
        for rows_half, target in (
            ((HALF_AA, HALF_AB)[half], device(da=(1, -1)[half])),
            ((HALF_BA, HALF_BB)[half], device(db=(1, -1)[half])),
        ):
            rows = rows_of(rows_half)
            step6[j].append(
                start(
                    gram.at[(3, 1)[half], j, rows, wide], gram.at[2, j, rows, wide], target
                )
            )

    direct, forward = {}, {}

    def mirrored_terms(slot, ref):
        return lax.dot_general(
            gram[slot, 3, :, body], slot_rows(ref, 3, slot), LEFT_TRANSPOSED,
            preferred_element_type=jnp.float32,
        )

    def once_mirrored(slot, first=False):
        terms = mirrored_terms(slot, xs)
        acc[...] = terms if first else acc[...] + terms

    def once_add(j, pieces):
        left = [gram[slot, j, rows_of(part), body] for slot, part in pieces]
        left = left[0] if len(left) == 1 else jnp.concatenate(left, axis=0)
        term = jnp.dot(left, xs[j], preferred_element_type=jnp.float32)
        rows = pl.ds(0, sum(part[1] for _, part in pieces))
        y_acc[rows, :] = term if j == 0 else y_acc[rows, :] + term

    def once(name, pieces):
        offset = 0
        for slot, part in pieces:
            place = place_of(slot, part)
            value = y_acc[pl.ds(offset, part[1]), :] + acc[place, :]
            offset += part[1]
            acc[place, :] = coef_linear * xs[0, place, :].astype(jnp.float32) + coef_cubic * value
            ys[0, place, :] = value.astype(jnp.bfloat16)
        first = [p for p in pieces if p[1][0] < PART_B[0]]
        second = [p for p in pieces if p[1][0] >= PART_B[0]]
        direct[name] = {}
        for ups, downs in ((first, second), (second, first)):
            for way, block, group in ((1, 3, ups), (-1, 1, downs)):
                for slot, part in group:
                    place = place_of(slot, part)
                    direct[name][way, slot, part] = start(
                        ys.at[0, place], ys.at[block, place], device(dz=way)
                    )

    def pass_on(name):
        forward[name] = []
        for (way, slot, part), copy in direct[name].items():
            if (part[0] < PART_B[0]) == (way == 1):
                received([copy])
                place = place_of(slot, part)
                block = 3 if way == 1 else 1
                forward[name].append(
                    start(ys.at[block, place], ys.at[2, place], device(dz=way))
                )

    def twice(j, last=False):
        def add(slot, carry):
            term = coef_quintic * jnp.dot(
                gram[slot, j, :, body], ys[j], preferred_element_type=jnp.float32
            )
            for part in (PART_A, PART_B):
                place = place_of(slot, part)
                value = acc[place, :] + term[part[0] : part[0] + part[1], :]
                if last:
                    o_ref[place, :] = (factor * value).astype(jnp.bfloat16)
                else:
                    acc[place, :] = value
            return carry

        lax.fori_loop(0, 4, add, 0)

    def twice_mirrored(slot):
        acc[...] += coef_quintic * mirrored_terms(slot, ys)

    slot_own = ((0, PART_A), (0, PART_B))
    slot_first = ((1, HALF_AA), (3, HALF_AA), (1, HALF_BA), (3, HALF_BA))
    slot_second = ((1, HALF_AB), (3, HALF_AB), (1, HALF_BB), (3, HALF_BB))
    slot_last = ((2, PART_A), (2, PART_B))

    for h in range(3):
        phase1(0, h)
    for h in range(3):
        phase2(0, h)
    phase3(0)
    received(from_next[0])
    phase1(1, 0)
    phase3_on(0)
    received(from_last[2])
    phase1(2, 0)
    phase2(1, 0)
    phase4(0)
    received(from_next[1])
    phase1(1, 1)
    received(from_last[1])
    received(from_last[3])
    phase2(2, 0)
    phase1(2, 1)
    spread_on(0)
    phase2(1, 1)
    phase2(2, 1)
    received(from_next[2])
    phase1(1, 2)
    phase1(2, 2)
    phase2(1, 2)
    phase3(1)
    received(from_last[0])
    phase2(2, 2)
    phase3_on(1)
    phase3(2)
    phase4(1)
    phase3_on(2)
    received(shared[1])
    spread(3)
    phase4(2)
    for slot in (2, 1):
        send_far(3, slot)
    for slot in (3, 0):
        send_far(1, slot)
    spread_on(3)
    spread(1)
    phase5(3, 0)
    phase5(3, 1)
    received(shared[2])
    spread(2)
    spread_on(1)
    received(step4_on[0])
    once_add(0, slot_own)
    once_mirrored(0, first=True)
    phase6(3, 0)
    spread_on(2)
    phase6(3, 1)
    received(step4_on[1])
    once_add(1, slot_own)
    phase5(0, 0)
    phase5(1, 0)
    once_mirrored(1)
    once_mirrored(3)
    phase5(2, 0)
    received(far)
    once_add(2, slot_own)
    phase5(0, 1)
    phase5(1, 1)
    phase5(2, 1)
    received(step6[3])
    once_mirrored(2)
    once("own", slot_own)
    for j in range(3):
        phase6(j, 0)
        if j == 2:
            pass_on("own")
        once_add(j, slot_first)
    once("first", slot_first)
    for j in range(3):
        phase6(j, 1)
        if j == 2:
            pass_on("first")
        once_add(j, slot_second)
    once("second", slot_second)
    for j in range(3):
        received(step6[j])
        once_add(j, slot_last)
    once("last", slot_last)
    pass_on("second")
    twice(0)
    for name in ("own", "first", "second"):
        received(direct[name].values())
    twice_mirrored(0)
    twice_mirrored(1)
    twice_mirrored(3)
    pass_on("last")
    received(direct["last"].values())
    twice_mirrored(2)
    twice(1)
    for name in ("own", "first", "second", "last"):
        received(forward[name])
    twice(2, last=True)
    sent(list(unsent))


def on_device(iterate):
    any_space = pl.BlockSpec(memory_space=pl.ANY)
    vmem = pl.BlockSpec(memory_space=pltpu.VMEM)
    bf16 = jnp.bfloat16
    return pl.pallas_call(
        kernel,
        out_shape=jax.ShapeDtypeStruct((BLOCK, DEPTH), bf16),
        in_specs=[any_space],
        out_specs=vmem,
        scratch_shapes=[
            pltpu.VMEM((4, BLOCK, DEPTH), bf16),
            pltpu.VMEM((2, 3, CHUNK, WIDE), bf16),
            pltpu.VMEM((2, CHUNK, FULL), bf16),
            pltpu.VMEM((2, CHUNK, WIDE), bf16),
            pltpu.VMEM((2, 2, CHUNK, WIDE), bf16),
            pltpu.VMEM((2, CHUNK, PIECE), bf16),
            pltpu.VMEM((2, 2, CHUNK, PIECE), bf16),
            pltpu.VMEM((CHUNK, PIECE), bf16),
            pltpu.VMEM((4, 4, CHUNK, FULL), bf16),
            pltpu.VMEM((4, BLOCK, DEPTH), bf16),
            pltpu.VMEM((BLOCK, DEPTH), jnp.float32),
            pltpu.VMEM((352, DEPTH), jnp.float32),
            pltpu.SemaphoreType.DMA,
            pltpu.SemaphoreType.DMA((COPIES,)),
            pltpu.SemaphoreType.DMA((COPIES,)),
        ],
        compiler_params=pltpu.CompilerParams(
            collective_id=0, has_side_effects=True, vmem_limit_bytes=63 * 2**20
        ),
        name="newton_schulz",
    )(iterate)


def solution(mesh):
    return jax.shard_map(
        on_device,
        mesh=mesh,
        in_specs=(P(("layer", "row"), "col"),),
        out_specs=P(("layer", "row"), "col"),
        check_vma=False,
    )
```

```python
import functools
import math

import jax
import jax.numpy as jnp
from jax import lax
from jax.experimental import pallas as pl
from jax.experimental.pallas import tpu as pltpu
from jax.sharding import PartitionSpec as P

M = 5376
N = 12288

coef_linear = 3.4445
coef_cubic = -4.775
coef_quintic = 2.0315
factor = 0.2 * math.sqrt(max(M, N))

BLOCK = 1344
CHUNK = 336
THIRDS = ((0, 512, 512), (512, 512, 512), (1024, 320, 384))
DEPTH = 768
WIDE = 1408
PIECE = 384
FULL = 4 * PIECE

PART_A = (0, 176)
PART_B = (176, 160)
HALF_AA = (0, 96)
HALF_AB = (96, 80)
HALF_BA = (176, 80)
HALF_BB = (256, 80)

TRANSPOSED = (((1,), (1,)), ((), ()))
LEFT_TRANSPOSED = (((0,), (0,)), ((), ()))
COPIES = 250


def rows_of(part):
    return pl.ds(part[0], part[1])


def kernel(
    x_hbm, o_ref, xs, send, summed, got_far, got_near, relayed, got_piece, handed, gram, ys, acc,
    y_acc, mirror_acc,
    local_sem, send_sem, recv_sem,
):
    layer = lax.axis_index("layer")
    row = lax.axis_index("row")
    col = lax.axis_index("col")
    px = lax.div(col, 4)
    py = lax.rem(col, 4)
    pa = px * (1 - layer) + py * layer
    pb = py * (1 - layer) + px * layer

    def ring(position, step):
        return lax.rem(position + (step + 4), 4)

    def device(da=0, db=0, dz=0):
        na, nb = ring(pa, da), ring(pb, db)
        nx = na * (1 - layer) + nb * layer
        ny = nb * (1 - layer) + na * layer
        return (layer, ring(row, dz), nx * 4 + ny)

    used = [0]

    def start(src, dst, target):
        index = used[0]
        used[0] += 1
        copy = pltpu.make_async_remote_copy(
            src_ref=src,
            dst_ref=dst,
            send_sem=send_sem.at[index],
            recv_sem=recv_sem.at[index],
            device_id=target,
            device_id_type=pl.DeviceIdType.MESH,
        )
        copy.start()
        unsent.append(copy)
        return copy

    unsent = []

    def sent(copies):
        for copy in copies:
            copy.wait_send()
            unsent[:] = [other for other in unsent if other is not copy]

    landed = []

    def received(copies):
        for copy in copies:
            if not any(other is copy for other in landed):
                landed.append(copy)
                copy.wait_recv()

    partners = [device(dz=1), device(dz=-1)]
    for step in (1, 2, 3):
        partners += [device(da=step), device(db=step)]
    barrier = pltpu.get_barrier_semaphore()
    for partner in partners:
        pl.semaphore_signal(
            barrier, inc=1, device_id=partner, device_id_type=pl.DeviceIdType.MESH
        )
    own = pltpu.make_async_copy(x_hbm, xs.at[0], local_sem)
    own.start()
    pl.semaphore_wait(barrier, len(partners))

    def place_of(slot, part):
        position = pa if part[0] < PART_B[0] else pb
        return pl.ds(pl.multiple_of(ring(position, slot) * CHUNK + part[0], 16), part[1])

    columns = [pl.ds(first, count) for first, count, _ in THIRDS]
    wide_columns = [pl.ds(first, count) for first, _, count in THIRDS]
    from_next, from_last = {}, {}

    def send_down(h):
        from_next[h] = [start(x_hbm.at[columns[h]], xs.at[1, columns[h]], device(dz=-1))]

    def send_up(slot):
        from_last[slot] = []
        for part in (PART_A, PART_B):
            place = place_of(slot, part)
            from_last[slot].append(start(x_hbm.at[place], xs.at[3, place], device(dz=1)))

    send_down(0)
    send_up(2)
    send_down(1)
    send_up(1)
    send_up(3)
    send_down(2)
    send_up(0)

    for k in range(2):
        summed[k, :, pl.ds(1280, FULL - 1280)] = jnp.zeros((CHUNK, FULL - 1280), jnp.bfloat16)
    own.wait()
    acc[...] = jnp.zeros((BLOCK, DEPTH), jnp.float32)

    far = []

    def send_far(j, slot):
        for part in (PART_A, PART_B):
            place = place_of(slot, part)
            way = device(dz=1) if j == 3 else device(dz=-1)
            far.append(start(xs.at[j, place], xs.at[2, place], way))

    def slot_rows(ref, j, slot):
        return jnp.concatenate(
            [ref[j, place_of(slot, PART_A), :], ref[j, place_of(slot, PART_B), :]], axis=0
        )

    def gram_terms(slot, j, h):
        left, right = (3, 1) if j == 2 else (0, j)
        return lax.dot_general(
            slot_rows(xs, left, slot), xs[right, columns[h], :], TRANSPOSED,
            preferred_element_type=jnp.float32,
        )

    buffer_set = {0: 0, 1: 1, 2: 0}
    from_buffer = {}
    step1, step2, step3, step3_on = {}, {}, {}, {}
    step4, step4_on, step5, step6 = {}, {}, {}, {}
    second_rings = (
        ((HALF_AA, HALF_AB), pb, lambda way: device(db=way)),
        ((HALF_BA, HALF_BB), pa, lambda way: device(da=way)),
    )
    body = pl.ds(0, BLOCK)
    wide = pl.ds(0, WIDE)

    def reuse(name, j):
        key = name, buffer_set[j]
        owner, copies = from_buffer.get(key, (j, []))
        if owner != j:
            sent(copies)
            copies = []
        from_buffer[key] = (j, copies)
        return copies

    def phase1(j, h):
        k = buffer_set[j]
        copies = reuse("far", j)
        send[k, 0, :, columns[h]] = gram_terms(2, j, h).astype(jnp.bfloat16)
        step1[j, h] = []
        for half, target in (
            (HALF_AA, device(da=1)),
            (HALF_BA, device(db=1)),
            (HALF_AB, device(da=-1)),
            (HALF_BB, device(db=-1)),
        ):
            rows = rows_of(half)
            step1[j, h].append(
                start(
                    send.at[k, 0, rows, wide_columns[h]],
                    got_far.at[k, rows, wide_columns[h]],
                    target,
                )
            )
        copies += step1[j, h]

    def phase2(j, h):
        k = buffer_set[j]
        received(step1[j, h])
        step2[j, h] = []
        for side, slot, added in ((1, 1, (HALF_AA, HALF_BA)), (2, 3, (HALF_AB, HALF_BB))):
            copies = reuse(side, j)
            terms = gram_terms(slot, j, h)
            for half in (HALF_AA, HALF_AB, HALF_BA, HALF_BB):
                rows = rows_of(half)
                value = terms[half[0] : half[0] + half[1], :]
                if half in added:
                    value = value + got_far[k, rows, columns[h]].astype(jnp.float32)
                send[k, side, rows, columns[h]] = value.astype(jnp.bfloat16)
            way = 1 if slot == 1 else -1
            for part, target in ((PART_A, device(da=way)), (PART_B, device(db=way))):
                rows = rows_of(part)
                copy = start(
                    send.at[k, side, rows, wide_columns[h]],
                    got_near.at[k, side - 1, rows, wide_columns[h]],
                    target,
                )
                copies.append(copy)
                step2[j, h].append(copy)

    def piece(position):
        return pl.ds(pl.multiple_of(position * PIECE, 128), PIECE)

    def phase3(j):
        k = buffer_set[j]
        copies = reuse("sum", j)
        for h in range(3):
            terms = gram_terms(0, j, h)
            received(step2[j, h])
            summed[k, :, columns[h]] = (
                terms
                + got_near[k, 0, :, columns[h]].astype(jnp.float32)
                + got_near[k, 1, :, columns[h]].astype(jnp.float32)
            ).astype(jnp.bfloat16)
        step3[j] = []
        for halves, position, ring_device in second_rings:
            place = piece(ring(position, 2))
            for half, way in zip(halves, (1, -1)):
                rows = rows_of(half)
                step3[j].append(
                    start(summed.at[k, rows, place], relayed.at[k, rows], ring_device(way))
                )
        copies += step3[j]

    def phase3_on(j):
        k = buffer_set[j]
        received(step3[j])
        step3_on[j] = []
        for (_, position, ring_device), part in zip(second_rings, (PART_A, PART_B)):
            for side, way in enumerate((1, -1)):
                place = piece(ring(position, way))
                half = second_rings[part == PART_B][0][side]
                rows = rows_of(half)
                summed[k, rows, place] = (
                    summed[k, rows, place].astype(jnp.float32)
                    + relayed[k, rows, :].astype(jnp.float32)
                ).astype(jnp.bfloat16)
                rows = rows_of(part)
                step3_on[j].append(
                    start(
                        summed.at[k, rows, place], got_piece.at[k, side, rows], ring_device(way)
                    )
                )
        from_buffer["sum", k][1].extend(step3_on[j])

    def spread(j):
        step4[j] = []
        for (_, position, ring_device), part in zip(second_rings, (PART_A, PART_B)):
            where = gram.at[0, j, rows_of(part), piece(position)]
            for way in (1, -1):
                step4[j].append(start(where, where, ring_device(way)))

    def spread_on(j):
        received(step4[j])
        step4_on[j] = []
        for halves, position, ring_device in second_rings:
            for half, way in zip(halves, (1, -1)):
                where = gram.at[0, j, rows_of(half), piece(ring(position, -way))]
                step4_on[j].append(start(where, where, ring_device(way)))

    def phase4(j):
        k = buffer_set[j]
        received(step3_on[j])
        for part, place in ((PART_A, pb), (PART_B, pa)):
            rows = rows_of(part)
            value = summed[k, rows, piece(place)].astype(jnp.float32)
            for side in range(2):
                value = value + got_piece[k, side, rows, :].astype(jnp.float32)
            value = value.astype(jnp.bfloat16)
            if j == 2:
                handed[rows, :] = value
            else:
                gram[0, j, rows, piece(place)] = value
        if j != 0:
            shared[j] = []
            for part, place in ((PART_A, pb), (PART_B, pa)):
                rows = rows_of(part)
                if j == 1:
                    src, theirs, way = gram.at[0, 1, rows, piece(place)], 3, 1
                else:
                    src, theirs, way = handed.at[rows], 2, -1
                shared[j].append(
                    start(src, gram.at[0, theirs, rows, piece(place)], device(dz=way))
                )
        if j == 0:
            spread(j)

    shared = {}

    def phase5(j, half):
        if half == 0:
            received(step4_on[j])
            step5[j] = []
        copies = []
        for rows_half, target_up, target_down in (
            ((HALF_AA, HALF_AB)[half], device(da=1), device(da=-1)),
            ((HALF_BA, HALF_BB)[half], device(db=1), device(db=-1)),
        ):
            rows = rows_of(rows_half)
            src = gram.at[0, j, rows, wide]
            copies.append(start(src, gram.at[3, j, rows, wide], target_up))
            copies.append(start(src, gram.at[1, j, rows, wide], target_down))
        step5[j].append(copies)

    def phase6(j, half):
        received(step5[j][half])
        if half == 0:
            step6[j] = []
        for rows_half, target in (
            ((HALF_AA, HALF_AB)[half], device(da=(1, -1)[half])),
            ((HALF_BA, HALF_BB)[half], device(db=(1, -1)[half])),
        ):
            rows = rows_of(rows_half)
            step6[j].append(
                start(
                    gram.at[(3, 1)[half], j, rows, wide], gram.at[2, j, rows, wide], target
                )
            )

    direct, forward = {}, {}

    def mirrored_terms(slot, ref, j=3):
        return lax.dot_general(
            gram[slot, j, :, body], slot_rows(ref, j, slot), LEFT_TRANSPOSED,
            preferred_element_type=jnp.float32,
        )

    def once_mirrored(slot, first=False):
        terms = mirrored_terms(slot, xs)
        mirror_acc[...] = terms if first else mirror_acc[...] + terms

    def once_add(j, pieces):
        left = [gram[slot, j, rows_of(part), body] for slot, part in pieces]
        left = left[0] if len(left) == 1 else jnp.concatenate(left, axis=0)
        term = jnp.dot(left, xs[j], preferred_element_type=jnp.float32)
        rows = pl.ds(0, sum(part[1] for _, part in pieces))
        y_acc[rows, :] = term if j == 0 else y_acc[rows, :] + term

    def once(name, pieces):
        offset = 0
        for slot, part in pieces:
            place = place_of(slot, part)
            value = y_acc[pl.ds(offset, part[1]), :] + mirror_acc[place, :]
            offset += part[1]
            acc[place, :] += coef_linear * xs[0, place, :].astype(jnp.float32) + coef_cubic * value
            ys[0, place, :] = value.astype(jnp.bfloat16)
        first = [p for p in pieces if p[1][0] < PART_B[0]]
        second = [p for p in pieces if p[1][0] >= PART_B[0]]
        direct[name] = {}
        for ups, downs in ((first, second), (second, first)):
            for way, block, group in ((1, 3, ups), (-1, 1, downs)):
                for slot, part in group:
                    place = place_of(slot, part)
                    direct[name][way, slot, part] = start(
                        ys.at[0, place], ys.at[block, place], device(dz=way)
                    )

    def pass_on(name):
        forward[name] = []
        for (way, slot, part), copy in direct[name].items():
            if (part[0] < PART_B[0]) == (way == 1):
                received([copy])
                place = place_of(slot, part)
                block = 3 if way == 1 else 1
                forward[name].append(
                    start(ys.at[block, place], ys.at[2, place], device(dz=way))
                )

    def twice(j, last=False):
        def add(slot, carry):
            term = coef_quintic * jnp.dot(
                gram[slot, j, :, body], ys[j], preferred_element_type=jnp.float32
            )
            for part in (PART_A, PART_B):
                place = place_of(slot, part)
                value = acc[place, :] + term[part[0] : part[0] + part[1], :]
                if last:
                    o_ref[place, :] = (factor * value).astype(jnp.bfloat16)
                else:
                    acc[place, :] = value
            return carry

        lax.fori_loop(0, 4, add, 0)

    def twice_mirrored(slot, j=3):
        acc[...] += coef_quintic * mirrored_terms(slot, ys, j)

    slot_own = ((0, PART_A), (0, PART_B))
    slot_first = ((1, HALF_AA), (3, HALF_AA), (1, HALF_BA), (3, HALF_BA))
    slot_second = ((1, HALF_AB), (3, HALF_AB), (1, HALF_BB), (3, HALF_BB))
    slot_last = ((2, PART_A), (2, PART_B))

    for h in range(3):
        phase1(0, h)
    for h in range(3):
        phase2(0, h)
    phase3(0)
    received(from_next[0])
    phase1(1, 0)
    phase3_on(0)
    received(from_last[2])
    phase1(2, 0)
    phase2(1, 0)
    phase4(0)
    received(from_next[1])
    phase1(1, 1)
    received(from_last[1])
    received(from_last[3])
    phase2(2, 0)
    phase1(2, 1)
    spread_on(0)
    phase2(1, 1)
    phase2(2, 1)
    received(from_next[2])
    phase1(1, 2)
    phase1(2, 2)
    phase2(1, 2)
    phase3(1)
    received(from_last[0])
    phase2(2, 2)
    phase3_on(1)
    phase3(2)
    phase5(0, 0)
    phase4(1)
    phase3_on(2)
    received(shared[1])
    spread(3)
    phase4(2)
    for slot in (2, 1):
        send_far(3, slot)
    for slot in (3, 0):
        send_far(1, slot)
    spread_on(3)
    spread(1)
    phase5(3, 0)
    phase5(3, 1)
    received(shared[2])
    spread(2)
    spread_on(1)
    received(step4_on[0])
    once_add(0, slot_own)
    once_mirrored(0, first=True)
    phase6(3, 0)
    spread_on(2)
    phase6(3, 1)
    received(step4_on[1])
    once_add(1, slot_own)
    phase5(1, 0)
    once_mirrored(1)
    once_mirrored(3)
    phase5(2, 0)
    received(far)
    once_add(2, slot_own)
    phase5(0, 1)
    phase5(1, 1)
    phase5(2, 1)
    received(step6[3])
    once_mirrored(2)
    once("own", slot_own)
    for j in range(3):
        phase6(j, 0)
        if j == 2:
            pass_on("own")
        once_add(j, slot_first)
    once("first", slot_first)
    twice_mirrored(0, 0)
    for j in range(3):
        phase6(j, 1)
        if j == 2:
            pass_on("first")
        once_add(j, slot_second)
    once("second", slot_second)
    received(direct["own"].values())
    twice_mirrored(0)
    twice_mirrored(1, 0)
    twice_mirrored(3, 0)
    for j in range(3):
        received(step6[j])
        once_add(j, slot_last)
    once("last", slot_last)
    pass_on("second")
    twice_mirrored(2, 0)
    for name in ("first", "second"):
        received(direct[name].values())
    twice_mirrored(1)
    twice_mirrored(3)
    pass_on("last")
    received(direct["last"].values())
    twice_mirrored(2)
    twice(1)
    for name in ("own", "first", "second", "last"):
        received(forward[name])
    twice(2, last=True)
    sent(list(unsent))


def on_device(iterate):
    any_space = pl.BlockSpec(memory_space=pl.ANY)
    vmem = pl.BlockSpec(memory_space=pltpu.VMEM)
    bf16 = jnp.bfloat16
    return pl.pallas_call(
        kernel,
        out_shape=jax.ShapeDtypeStruct((BLOCK, DEPTH), bf16),
        in_specs=[any_space],
        out_specs=vmem,
        scratch_shapes=[
            pltpu.VMEM((4, BLOCK, DEPTH), bf16),
            pltpu.VMEM((2, 3, CHUNK, WIDE), bf16),
            pltpu.VMEM((2, CHUNK, FULL), bf16),
            pltpu.VMEM((2, CHUNK, WIDE), bf16),
            pltpu.VMEM((2, 2, CHUNK, WIDE), bf16),
            pltpu.VMEM((2, CHUNK, PIECE), bf16),
            pltpu.VMEM((2, 2, CHUNK, PIECE), bf16),
            pltpu.VMEM((CHUNK, PIECE), bf16),
            pltpu.VMEM((4, 4, CHUNK, FULL), bf16),
            pltpu.VMEM((4, BLOCK, DEPTH), bf16),
            pltpu.VMEM((BLOCK, DEPTH), jnp.float32),
            pltpu.VMEM((352, DEPTH), jnp.float32),
            pltpu.VMEM((BLOCK, DEPTH), jnp.float32),
            pltpu.SemaphoreType.DMA,
            pltpu.SemaphoreType.DMA((COPIES,)),
            pltpu.SemaphoreType.DMA((COPIES,)),
        ],
        compiler_params=pltpu.CompilerParams(
            collective_id=0, has_side_effects=True, vmem_limit_bytes=63 * 2**20
        ),
        name="newton_schulz",
    )(iterate)


def solution(mesh):
    return jax.shard_map(
        on_device,
        mesh=mesh,
        in_specs=(P(("layer", "row"), "col"),),
        out_specs=P(("layer", "row"), "col"),
        check_vma=False,
    )
```
